512 devices in a mesh: dp: 16 (over y, x), seq: 32 (over z, core).
Axes of the slice: x: 4, y: 4, z: 16, core: 2. Of those that a mesh axis runs over, the one named last changes fastest.
Arguments:
- tokens: bfloat16 [4096, 4096], P('seq'), may hold values from -6 to 6
- w_in: bfloat16 [4096, 20608], P('seq', 'dp'), may hold values from -0.09375 to 0.09375
- conv_weight: float32 [4, 12288], P(None, 'dp'), may hold values from -0.8 to 0.8
- conv_bias: float32 [12288], P('dp'), may hold values from -0.5 to 0.5
- dt_bias: float32 [128], P('dp'), may hold values from -2 to 1
- decay_rate: float32 [128], P('dp'), may hold values from 1e-06 to 0.3
- skip_gain: float32 [128], P('dp'), may hold values from 0.5 to 1.5
- norm_gain: float32 [8192], P('dp'), may hold values from 0.5 to 1.5
- w_out: bfloat16 [8192, 4096], P('dp', 'seq'), may hold values from -0.0625 to 0.0625
Outputs:
- mixed: bfloat16 [4096, 4096], P('seq', 'dp')
The draws below stay inside these ranges and needn't reach their ends.
All inputs are finite; a program needn't handle non-finite values.
Results may differ from the reference program's by a relative error of at most 0.025.
Values may be sent and summed in bfloat16 or wider, within the bound.
A program may use at most 64 MiB of HBM per device.

```python
import math
import jax
import jax.numpy as jnp
from jax import lax

D = 4096
HEADS = 128
GROUPS = 16
P_SIZE = 64
N = 128
KCONV = 4
XG = 768
CG = 1288
E = 8192
LENGTH = 4096
N_DP = 16


def shard_levels(key, extent, pieces, least, top_value):
    gain, own = 1.0, jax.random.fold_in(key, 6)
    for dim, shards_of in pieces:
        steps = jnp.exp(jax.random.uniform(jax.random.fold_in(own, dim), (shards_of,), jnp.float32, least / len(pieces), top_value / len(pieces)))
        gain = gain * jnp.repeat(steps, extent[dim] // shards_of).reshape([-1 if axis == dim else 1 for axis in range(len(extent))])
    return gain


def scatter_about(stream_key, dims, width, limit, cuts=(), dtype=jnp.bfloat16):
    values = width * jax.random.normal(stream_key, dims, jnp.float32)
    if cuts:
        values = values * shard_levels(stream_key, dims, cuts, -0.22, 0.18)
    return jnp.clip(values, -limit, limit).astype(dtype)


def setup_inputs(seed: int = 0) -> dict:
    key_list = jax.random.split(jax.random.key(seed), 10)
    tokens = scatter_about(key_list[0], (LENGTH, D), 1.0, 6.0, ((0, 32),))
    w_in = scatter_about(key_list[1], (D, GROUPS * CG), D ** -0.5, 0.09375, ((0, 32), (1, 16)))
    conv_weight = jnp.clip(jax.random.uniform(key_list[2], (KCONV, GROUPS * XG), jnp.float32, -0.8, 0.8) * shard_levels(key_list[2], (KCONV, GROUPS * XG), ((1, 16),), -0.4, 0.0), -0.8, 0.8)
    conv_bias = jnp.clip(jax.random.uniform(key_list[3], (GROUPS * XG,), jnp.float32, -0.5, 0.5) * shard_levels(key_list[3], (GROUPS * XG,), ((0, 16),), -0.4, 0.0), -0.5, 0.5)
    dt_bias = jnp.clip(-2.0 + 3.0 * jax.random.uniform(key_list[4], (HEADS,), jnp.float32) ** shard_levels(key_list[4], (HEADS,), ((0, 16),), -0.2, 0.2), -2.0, 1.0)
    decay_rate = jnp.clip(jnp.exp(math.log(0.3) - 12.611538 * jax.random.uniform(key_list[5], (HEADS,), jnp.float32) ** shard_levels(key_list[5], (HEADS,), ((0, 16),), -0.2, 0.2)), 9.999999974752427e-07, 0.3)
    skip_gain = jnp.clip(0.5 + 1.0 * jax.random.uniform(key_list[6], (HEADS,), jnp.float32) ** shard_levels(key_list[6], (HEADS,), ((0, 16),), -0.2, 0.2), 0.5, 1.5)
    norm_gain = jnp.clip(1.0 + 0.1 * jax.random.normal(key_list[7], (E,), jnp.float32), 0.5, 1.5)
    w_out = scatter_about(key_list[8], (E, D), E ** -0.5, 0.0625, ((0, 16), (1, 32)))
    return dict(tokens=tokens, w_in=w_in, conv_weight=conv_weight, conv_bias=conv_bias, dt_bias=dt_bias, decay_rate=decay_rate, skip_gain=skip_gain, norm_gain=norm_gain, w_out=w_out)


def reference(tokens, w_in, conv_weight, conv_bias, dt_bias, decay_rate, skip_gain, norm_gain, w_out):
    length = tokens.shape[0]
    hg = HEADS // GROUPS
    xg = hg * P_SIZE + 2 * N
    proj = jnp.dot(tokens, w_in, preferred_element_type=jnp.float32).astype(jnp.bfloat16)
    proj = proj.reshape(length, GROUPS, 2 * hg * P_SIZE + 2 * N + hg)
    zpart = proj[:, :, :hg * P_SIZE].astype(jnp.float32)
    xbc = proj[:, :, hg * P_SIZE:hg * P_SIZE + xg].astype(jnp.float32)
    draw = proj[:, :, hg * P_SIZE + xg:].astype(jnp.float32).reshape(length, HEADS)
    padded = jnp.concatenate([jnp.zeros((KCONV - 1, GROUPS, xg), jnp.float32), xbc], axis=0)
    taps = conv_weight.reshape(KCONV, GROUPS, xg)
    conv = jnp.zeros((length, GROUPS, xg), jnp.float32) + conv_bias.reshape(GROUPS, xg)
    for k in range(KCONV):
        conv = conv + taps[k] * padded[k:k + length]
    act = jax.nn.silu(conv)
    xs = act[:, :, :hg * P_SIZE].reshape(length, HEADS, P_SIZE)
    bmat = jnp.repeat(act[:, :, hg * P_SIZE:hg * P_SIZE + N], hg, axis=1)
    cmat = jnp.repeat(act[:, :, hg * P_SIZE + N:], hg, axis=1)
    dt = jax.nn.softplus(draw + dt_bias)
    decay = jnp.exp(-dt * decay_rate)

    def advance(state, inputs):
        x_t, b_t, c_t, dt_t, d_t = inputs
        state = d_t[:, None, None] * state + dt_t[:, None, None] * b_t[:, :, None] * x_t[:, None, :]
        y_t = jnp.einsum('hn,hnp->hp', c_t, state, precision=lax.Precision.HIGHEST)
        return (state, y_t)
    start = jnp.zeros((HEADS, N, P_SIZE), jnp.float32)
    _, ys = lax.scan(advance, start, (xs, bmat, cmat, dt, decay))
    ys = ys + skip_gain[None, :, None] * xs
    gated = ys.reshape(length, GROUPS, hg * P_SIZE) * jax.nn.silu(zpart)
    meansq = lax.optimization_barrier(jnp.mean(gated * gated, axis=2, keepdims=True))
    normed = gated * lax.rsqrt(meansq + 1e-05) * norm_gain.reshape(GROUPS, hg * P_SIZE)
    normed = normed.reshape(length, HEADS * P_SIZE).astype(jnp.bfloat16)
    part = HEADS * P_SIZE // N_DP
    total = jnp.zeros((length, D), jnp.float32)
    for index in range(N_DP):
        term = jnp.dot(normed[:, index * part:(index + 1) * part], w_out[index * part:(index + 1) * part], preferred_element_type=jnp.float32)
        term = lax.optimization_barrier(term.astype(jnp.bfloat16))
        total = total + term.astype(jnp.float32)
    return total.astype(jnp.bfloat16)
```

```python
import functools

import jax
import jax.numpy as jnp
from jax import lax
from jax.experimental import pallas as pl
from jax.experimental.pallas import tpu as pltpu
from jax.sharding import PartitionSpec as P

P_SIZE = 64
N = 128
KCONV = 4
BLOCK = 128
HG = 8
XG = 768
CG = 1288
ZC = 512
HALO = 16
AROWS = 16 + XG
BF = jnp.bfloat16
F32 = jnp.float32
MESH = pl.DeviceIdType.MESH
VMEM_LIMIT = 56 * 1024 * 1024

A_PARTS = ((0, 400), (400, 384))
W_PARTS = ((0, 256), (256, 256))


class Ring:
    def __init__(self, buf, parts, chips, core, right, left, sib, sems):
        self.buf, self.parts, self.chips, self.core = buf, parts, chips, core
        self.right, self.left, self.sib = right, left, sib
        self.recv, self.send_r, self.send_l, self.srecv, self.ssend = sems
        self.half = chips // 2

    def reach(self, h, going_right):
        return self.half if (h == 0) == going_right else self.half - 1

    def _hop(self, q, to, h, going_right):
        lo, size = self.parts[h]
        return pltpu.make_async_remote_copy(
            src_ref=self.buf.at[q, self.core, pl.ds(lo, size)],
            dst_ref=self.buf.at[to, self.core, pl.ds(lo, size)],
            send_sem=(self.send_r if going_right else self.send_l).at[q, h],
            recv_sem=self.recv.at[to, h],
            device_id=self.right if going_right else self.left,
            device_id_type=MESH,
        )

    def _share(self, q):
        return pltpu.make_async_remote_copy(
            src_ref=self.buf.at[q, self.core],
            dst_ref=self.buf.at[q, self.core],
            send_sem=self.ssend.at[q],
            recv_sem=self.srecv.at[q],
            device_id=self.sib,
            device_id_type=MESH,
        )

    def begin(self):
        for h in range(2):
            self._hop(0, 1, h, True).start()
            self._hop(0, self.chips - 1, h, False).start()
        self._share(0).start()

    def step(self, k, last=False, final=False):
        z = self.chips
        for h in range(2):
            for going_right in (True, False):
                if final and self.reach(h, going_right) < self.half:
                    continue
                q = k if going_right else z - k
                self._hop(q, q, h, going_right).wait_recv()
                if final or (last and self.reach(h, going_right) < self.half):
                    continue
                self._hop(q, q + 1 if going_right else q - 1, h, going_right).start()
        self._share(k).start()
        if not final:
            self._share(z - k).start()

    def shared(self, q):
        self._share(q).wait_recv()

    def drain(self):
        z, half = self.chips, self.half

        def sends(q, going_right, hs):
            for h in hs:
                self._hop(q, q, h, going_right).wait_send()

        @pl.loop(0, half - 1)
        def _(k):
            sends(k, True, (0, 1))
            sends(lax.rem(z - k, z), False, (0, 1))

        sends(half - 1, True, (0,))
        sends(half + 1, False, (1,))

        @pl.loop(0, z)
        def _(q):
            self._share(q).wait_send()


def ring_sems(chips):
    dma = pltpu.SemaphoreType.DMA
    return [dma((chips, 2)), dma((chips, 2)), dma((chips, 2)), dma((chips,)), dma((chips,))]


def proj_kernel(chips, tok_hbm, win_ref, proj_ref, dt_ref, tokx, buf_a, buf_z, acc, acc_dt, local_sem, halo_send, halo_recv, *sems):
    d, s = lax.axis_index("dp"), lax.axis_index("seq")
    n_seq = 2 * chips
    core, z = lax.rem(s, 2), s // 2
    right = (d, lax.rem(s + 2, n_seq))
    left = (d, lax.rem(s + n_seq - 2, n_seq))
    sib = (d, s + 1 - 2 * core)
    nxt = (d, lax.rem(s + 1, n_seq))
    prv = (d, lax.rem(s + n_seq - 1, n_seq))

    barrier = pltpu.get_barrier_semaphore()

    @pl.loop(1, n_seq)
    def _(k):
        pl.semaphore_signal(barrier, inc=1, device_id=(d, lax.rem(s + k, n_seq)), device_id_type=MESH)

    own = pltpu.make_async_copy(tok_hbm, tokx.at[pl.ds(HALO, BLOCK)], local_sem)
    own.start()
    buf_a[0, core, 0:16] = jnp.zeros((16, N), BF)
    dtw = jnp.concatenate([win_ref[:, ZC + XG : CG].astype(F32), jnp.zeros((BLOCK, N - HG), F32)], axis=1)
    buf_a[0, core, 0:16] = dtw.T[0:16].astype(BF)
    for t in range(XG // N):
        buf_a[0, core, 16 + t * N : 16 + (t + 1) * N] = win_ref[:, ZC + t * N : ZC + (t + 1) * N]
    for t in range(ZC // N):
        buf_z[0, core, t * N : (t + 1) * N] = win_ref[:, t * N : (t + 1) * N]
    acc[...] = jnp.zeros_like(acc)
    acc_dt[...] = jnp.zeros_like(acc_dt)
    pl.semaphore_wait(barrier, n_seq - 1)

    ring_a = Ring(buf_a, A_PARTS, chips, core, right, left, sib, sems[0:5])
    ring_z = Ring(buf_z, W_PARTS, chips, core, right, left, sib, sems[5:10])
    ring_a.begin()
    halo = pltpu.make_async_remote_copy(
        src_ref=tok_hbm.at[pl.ds(BLOCK - HALO, HALO)],
        dst_ref=tokx.at[pl.ds(0, HALO)],
        send_sem=halo_send,
        recv_sem=halo_recv,
        device_id=nxt,
        device_id_type=MESH,
    )
    halo.start()
    own.wait()
    halo.wait_recv()

    def tokens_of(q):
        owner = lax.rem(z - q + chips, chips)
        return tokx[:, pl.ds(pl.multiple_of(owner * 2 * N, 2 * N), 2 * N)]

    def two_tiles(buf, q, row):
        left_tile = buf[q, :, row : row + N].reshape(2 * N, N)
        right_tile = buf[q, :, row + N : row + 2 * N].reshape(2 * N, N)
        return jnp.concatenate([left_tile, right_tile], axis=1)

    def use_a(q):
        t = tokens_of(q)
        w = jnp.concatenate([buf_a[q, 0, 0:16], buf_a[q, 1, 0:16]], axis=1)
        acc_dt[...] += lax.dot_general(t, w, (((1,), (1,)), ((), ())), preferred_element_type=F32)
        for i in range(XG // (2 * N)):
            cols = pl.ds(ZC + i * 2 * N, 2 * N)
            acc[:, cols] += jnp.dot(t, two_tiles(buf_a, q, 16 + i * 2 * N), preferred_element_type=F32)

    def use_z(q):
        t = tokens_of(q)
        for i in range(ZC // (2 * N)):
            cols = pl.ds(i * 2 * N, 2 * N)
            acc[:, cols] += jnp.dot(t, two_tiles(buf_z, q, i * 2 * N), preferred_element_type=F32)

    half = chips // 2

    def run(ring, use, after_last):
        ring.shared(0)
        use(0)

        def both(k):
            ring.shared(k)
            use(k)
            ring.shared(chips - k)
            use(chips - k)

        @pl.loop(1, half - 1)
        def _(k):
            ring.step(k)

            @pl.when(k > 1)
            def _():
                both(k - 1)

        ring.step(half - 1, last=True)
        after_last()
        if half > 2:
            both(half - 2)
        both(half - 1)
        ring.step(half, final=True)
        ring.shared(half)
        use(half)

    run(ring_a, use_a, ring_z.begin)
    run(ring_z, use_z, lambda: None)
    proj_ref[...] = acc[...].astype(BF)
    dt_ref[...] = acc_dt[...].astype(BF)
    halo.wait_send()
    ring_a.drain()
    ring_z.drain()


def project(tokens, w_in, chips):
    rows = HALO + BLOCK
    dma = pltpu.SemaphoreType.DMA
    return pl.pallas_call(
        functools.partial(proj_kernel, chips),
        out_shape=(jax.ShapeDtypeStruct((rows, ZC + XG), BF), jax.ShapeDtypeStruct((rows, 16), BF)),
        in_specs=[pl.BlockSpec(memory_space=pl.ANY), pl.BlockSpec(memory_space=pltpu.VMEM)],
        out_specs=(pl.BlockSpec(memory_space=pltpu.VMEM), pl.BlockSpec(memory_space=pltpu.VMEM)),
        scratch_shapes=[
            pltpu.VMEM((rows, tokens.shape[1]), BF),
            pltpu.VMEM((chips, 2, AROWS, N), BF),
            pltpu.VMEM((chips, 2, ZC, N), BF),
            pltpu.VMEM((rows, ZC + XG), F32),
            pltpu.VMEM((rows, 16), F32),
            dma,
            dma,
            dma,
            *ring_sems(chips),
            *ring_sems(chips),
        ],
        compiler_params=pltpu.CompilerParams(
            collective_id=0, has_side_effects=True, vmem_limit_bytes=VMEM_LIMIT
        ),
    )(tokens, w_in)


def from_behind(block, axis, distance):
    devices = range(lax.axis_size(axis))
    route = [(i - distance, i) for i in devices if i - distance in devices]
    return lax.ppermute(block, axis, route)


def combine(earlier, later):
    return (earlier[0] * later[0], later[0][:, :, None, None] * earlier[1] + later[1])


def per_device(
    tokens, w_in, conv_weight, conv_bias, dt_bias, decay_rate, skip_gain, norm_gain, w_out
):
    rows = tokens.shape[0]
    heads_dev = decay_rate.shape[0]
    groups_dev = heads_dev // HG
    blocks = rows // BLOCK
    projx, draw = project(tokens, w_in, lax.axis_size("seq") // 2)
    draw = draw[HALO:, :HG].astype(jnp.float32)
    first = lax.axis_index("seq") == 0
    rim = jnp.where(first, 0, projx[HALO - 3 : HALO, ZC:])
    xbc = projx[HALO:, ZC:]
    padded = jnp.concatenate([rim, xbc], axis=0).astype(jnp.float32)[:, None]
    zpart = projx[HALO:, None, :ZC].astype(jnp.float32)
    taps = conv_weight.reshape(KCONV, groups_dev, XG)
    conv = jnp.zeros((rows, groups_dev, XG), jnp.float32) + conv_bias.reshape(groups_dev, XG)
    for k in range(KCONV):
        conv = conv + taps[k] * padded[k : k + rows]
    act = jax.nn.silu(conv)
    xs = act[:, :, : HG * P_SIZE].reshape(blocks, BLOCK, groups_dev, HG, P_SIZE)
    bmat = act[:, :, HG * P_SIZE : HG * P_SIZE + N].reshape(blocks, BLOCK, groups_dev, N)
    cmat = act[:, :, HG * P_SIZE + N :].reshape(blocks, BLOCK, groups_dev, N)
    dt = jax.nn.softplus(draw + dt_bias)
    logdec = (-dt * decay_rate).reshape(blocks, BLOCK, groups_dev, HG)
    dtq = dt.reshape(blocks, BLOCK, groups_dev, HG)
    cum = jnp.cumsum(logdec, axis=1)
    scores = jnp.einsum("btgn,bsgn->btsg", cmat, bmat, precision=lax.Precision.HIGHEST)
    later = lax.broadcasted_iota(jnp.int32, (BLOCK, BLOCK), 0) >= lax.broadcasted_iota(
        jnp.int32, (BLOCK, BLOCK), 1
    )
    later = later[None, :, :, None, None]
    gap = cum[:, :, None] - cum[:, None, :]
    weights = jnp.where(later, jnp.exp(jnp.where(later, gap, 0.0)), 0.0)
    mixing = scores[..., None] * weights * dtq[:, None]
    ydiag = jnp.einsum("btsgh,bsghp->btghp", mixing, xs, precision=lax.Precision.HIGHEST)
    tail = jnp.exp(cum[:, -1:] - cum) * dtq
    block_state = jnp.einsum(
        "bsgh,bsgn,bsghp->bghnp", tail, bmat, xs, precision=lax.Precision.HIGHEST
    )
    block_decay = jnp.exp(cum[:, -1])

    def gather_blocks(carry, item):
        return (combine(carry, item), carry)

    unit = (
        jnp.ones((groups_dev, HG), jnp.float32),
        jnp.zeros((groups_dev, HG, N, P_SIZE), jnp.float32),
    )
    (dev_decay, dev_state), (pre_decay, pre_state) = lax.scan(
        gather_blocks, unit, (block_decay, block_state)
    )

    def relay(step, incoming):
        outgoing = dev_decay[:, :, None, None] * incoming + dev_state
        return from_behind(outgoing.astype(jnp.bfloat16), "seq", 1).astype(outgoing.dtype)

    incoming = lax.fori_loop(
        0, lax.axis_size("seq") - 1, relay, jnp.zeros((groups_dev, HG, N, P_SIZE), jnp.float32)
    )
    block_in = pre_decay[:, :, :, None, None] * incoming[None] + pre_state
    yoff = jnp.einsum("btgn,bghnp->btghp", cmat, block_in, precision=lax.Precision.HIGHEST)
    yoff = yoff * jnp.exp(cum)[..., None]
    ys = ydiag + yoff + skip_gain.reshape(groups_dev, HG)[None, None, :, :, None] * xs
    gated = ys.reshape(rows, groups_dev, HG * P_SIZE) * jax.nn.silu(zpart)
    meansq = jnp.mean(gated * gated, axis=2, keepdims=True)
    normed = gated * lax.rsqrt(meansq + 1e-05) * norm_gain.reshape(groups_dev, HG * P_SIZE)
    normed = normed.reshape(rows, heads_dev * P_SIZE).astype(jnp.bfloat16)
    terms = jnp.dot(
        normed, lax.all_gather(w_out, "seq", axis=1, tiled=True), preferred_element_type=jnp.float32
    )
    return lax.psum_scatter(terms.astype(jnp.bfloat16), "dp", scatter_dimension=1, tiled=True)


def solution(mesh):
    placed = (
        P("seq", None),
        P("seq", "dp"),
        P(None, "dp"),
        P("dp"),
        P("dp"),
        P("dp"),
        P("dp"),
        P("dp"),
        P("dp", "seq"),
    )
    return jax.shard_map(
        per_device, mesh=mesh, in_specs=placed, out_specs=P("seq", "dp"), check_vma=False
    )
```

```python
import functools

import jax
import jax.numpy as jnp
from jax import lax
from jax.experimental import pallas as pl
from jax.experimental.pallas import tpu as pltpu
from jax.sharding import PartitionSpec as P

P_SIZE = 64
N = 128
KCONV = 4
BLOCK = 128
HG = 8
XG = 768
CG = 1288
ZC = 512
HALO = 16
AROWS = 16 + XG
XT = ZC // N
BF = jnp.bfloat16
F32 = jnp.float32
MESH = pl.DeviceIdType.MESH
HIGHEST = lax.Precision.HIGHEST
VMEM_LIMIT = 56 * 1024 * 1024

A_PARTS = ((0, 400), (400, 384))
W_PARTS = ((0, 256), (256, 256))


class Ring:
    def __init__(self, buf, parts, chips, core, right, left, sib, sems):
        self.buf, self.parts, self.chips, self.core = buf, parts, chips, core
        self.right, self.left, self.sib = right, left, sib
        self.recv, self.send_r, self.send_l, self.srecv, self.ssend = sems
        self.half = chips // 2

    def reach(self, h, going_right):
        return self.half if (h == 0) == going_right else self.half - 1

    def _hop(self, q, to, h, going_right):
        lo, size = self.parts[h]
        return pltpu.make_async_remote_copy(
            src_ref=self.buf.at[q, self.core, pl.ds(lo, size)],
            dst_ref=self.buf.at[to, self.core, pl.ds(lo, size)],
            send_sem=(self.send_r if going_right else self.send_l).at[q, h],
            recv_sem=self.recv.at[to, h],
            device_id=self.right if going_right else self.left,
            device_id_type=MESH,
        )

    def _share(self, q):
        return pltpu.make_async_remote_copy(
            src_ref=self.buf.at[q, self.core],
            dst_ref=self.buf.at[q, self.core],
            send_sem=self.ssend.at[q],
            recv_sem=self.srecv.at[q],
            device_id=self.sib,
            device_id_type=MESH,
        )

    def begin(self):
        for h in range(2):
            self._hop(0, 1, h, True).start()
            self._hop(0, self.chips - 1, h, False).start()
        self._share(0).start()

    def step(self, k, last=False, final=False):
        z = self.chips
        for h in range(2):
            for going_right in (True, False):
                if final and self.reach(h, going_right) < self.half:
                    continue
                q = k if going_right else z - k
                self._hop(q, q, h, going_right).wait_recv()
                if final or (last and self.reach(h, going_right) < self.half):
                    continue
                self._hop(q, q + 1 if going_right else q - 1, h, going_right).start()
        self._share(k).start()
        if not final:
            self._share(z - k).start()

    def at(self, k):
        self.step(k, last=k == self.half - 1, final=k == self.half)

    def shared(self, q):
        self._share(q).wait_recv()

    def drain(self):
        z, half = self.chips, self.half

        def sends(q, going_right, hs):
            for h in hs:
                self._hop(q, q, h, going_right).wait_send()

        @pl.loop(0, half - 1)
        def _(k):
            sends(k, True, (0, 1))
            sends(lax.rem(z - k, z), False, (0, 1))

        sends(half - 1, True, (0,))
        sends(half + 1, False, (1,))

        @pl.loop(0, z)
        def _(q):
            self._share(q).wait_send()


def ring_sems(chips):
    dma = pltpu.SemaphoreType.DMA
    return [dma((chips, 2)), dma((chips, 2)), dma((chips, 2)), dma((chips,)), dma((chips,))]


class Exchange:
    def __init__(self, out, inn, chips, z, peer, send, recv):
        self.out, self.inn, self.chips, self.z, self.peer = out, inn, chips, z, peer
        self.send, self.recv = send, recv
        half = chips // 2
        self.order = [half] + [k for j in range(1, half) for k in (half - j, half + j)]

    def _copy(self, o, slot):
        return pltpu.make_async_remote_copy(
            src_ref=self.out.at[o],
            dst_ref=self.inn.at[slot],
            send_sem=self.send.at[o],
            recv_sem=self.recv.at[slot],
            device_id=self.peer(o),
            device_id_type=MESH,
        )

    def begin(self):
        for k in self.order:
            self._copy(lax.rem(self.z + k, self.chips), self.z).start()
        self.inn[self.z] = self.out[self.z]

    def arrive(self):
        for k in reversed(self.order):
            q = lax.rem(self.z + k, self.chips)
            self._copy(q, q).wait_recv()

    def drain(self):
        for k in self.order:
            q = lax.rem(self.z + k, self.chips)
            self._copy(q, q).wait_send()


def silu(v):
    return v / (1.0 + jnp.exp(-v))


def two_parts(row):
    shape = (16, row.shape[1])
    high = row.astype(BF).astype(F32)
    low = row - high
    at = lax.broadcasted_iota(jnp.int32, shape, 0)
    high, low = jnp.broadcast_to(high, shape), jnp.broadcast_to(low, shape)
    return jnp.where(at == 0, high, jnp.where(at == 1, low, 0.0)).astype(BF)


def one_row(tile):
    tile = tile.astype(F32)
    return tile[0:1] + tile[1:2]


def head_lanes(values, j):
    shape = (values.shape[0], N)
    lane = lax.broadcasted_iota(jnp.int32, shape, 1)
    first = jnp.broadcast_to(values[:, 2 * j : 2 * j + 1], shape)
    second = jnp.broadcast_to(values[:, 2 * j + 1 : 2 * j + 2], shape)
    return jnp.where(lane < P_SIZE, first, second)


def batches(half):
    if half < 4:
        return [(0, half - 1), (half, half)]
    return [(0, half // 2), (half // 2 + 1, half - 2), (half - 1, half)]


def mixer_kernel(
    chips, n_dp,
    tok_hbm, win_ref, taps_ref, cbias_ref, dtb_ref, rate_ref, skip_ref, gain_ref, wout_ref,
    out_ref,
    tokx, buf_a, buf_z, buf_o, acc, acc_dt, xf, x1_out, x1_in, st_out, st_in, hin_out, hin_in,
    x2_out, hfull, normed, t_out, r_in,
    local_sem, halo_send, halo_recv, x1_send, x1_recv, x2_send, x2_recv,
    e1_send, e1_recv, e2_send, e2_recv, rs_send, rs_recv, *sems,
):
    d, s = lax.axis_index("dp"), lax.axis_index("seq")
    n_seq = 2 * chips
    half = chips // 2
    core, z = lax.rem(s, 2), s // 2
    right = (d, lax.rem(s + 2, n_seq))
    left = (d, lax.rem(s + n_seq - 2, n_seq))
    sib = (d, s + 1 - 2 * core)
    nxt = (d, lax.rem(s + 1, n_seq))
    odd = (d, lax.rem(s + n_seq - 1 + 2 * core, n_seq))
    tile_rows = 2 * N // chips

    barrier = pltpu.get_barrier_semaphore()

    def greet(device):
        pl.semaphore_signal(barrier, inc=1, device_id=device, device_id_type=MESH)

    @pl.loop(1, chips)
    def _(k):
        greet((d, lax.rem(s + 2 * k, n_seq)))

    @pl.loop(1, n_dp)
    def _(k):
        greet((lax.rem(d + k, n_dp), s))

    greet(sib)
    greet(odd)

    own = pltpu.make_async_copy(tok_hbm, tokx.at[pl.ds(HALO, BLOCK)], local_sem)
    own.start()
    dtw = jnp.concatenate([win_ref[:, ZC + XG : CG].astype(F32), jnp.zeros((BLOCK, N - HG), F32)], axis=1)
    buf_a[0, core, 0:16] = dtw.T[0:16].astype(BF)
    for t in range(XG // N):
        buf_a[0, core, 16 + t * N : 16 + (t + 1) * N] = win_ref[:, ZC + t * N : ZC + (t + 1) * N]
    for t in range(XT):
        buf_z[0, core, t * N : (t + 1) * N] = win_ref[:, t * N : (t + 1) * N]
    buf_o[0, core] = wout_ref[...]
    acc[...] = jnp.zeros_like(acc)
    acc_dt[...] = jnp.zeros_like(acc_dt)
    pl.semaphore_wait(barrier, chips + n_dp)

    ring_a = Ring(buf_a, A_PARTS, chips, core, right, left, sib, sems[0:5])
    ring_z = Ring(buf_z, W_PARTS, chips, core, right, left, sib, sems[5:10])
    ring_o = Ring(buf_o, W_PARTS, chips, core, right, left, sib, sems[10:15])
    ring_a.begin()
    halo = pltpu.make_async_remote_copy(
        src_ref=tok_hbm.at[pl.ds(BLOCK - HALO, HALO)],
        dst_ref=tokx.at[pl.ds(0, HALO)],
        send_sem=halo_send,
        recv_sem=halo_recv,
        device_id=nxt,
        device_id_type=MESH,
    )
    halo.start()
    own.wait()
    halo.wait_recv()

    def columns_of(q):
        owner = lax.rem(z - q + chips, chips)
        return pl.ds(pl.multiple_of(owner * 2 * N, 2 * N), 2 * N)

    def two_tiles(buf, q, row):
        left_tile = buf[q, :, row : row + N].reshape(2 * N, N)
        right_tile = buf[q, :, row + N : row + 2 * N].reshape(2 * N, N)
        return jnp.concatenate([left_tile, right_tile], axis=1)

    def use_a(q):
        ring_a.shared(q)
        t = tokx[:, columns_of(q)]
        w = jnp.concatenate([buf_a[q, 0, 0:16], buf_a[q, 1, 0:16]], axis=1)
        acc_dt[...] += lax.dot_general(t, w, (((1,), (1,)), ((), ())), preferred_element_type=F32)
        for i in range(XG // (2 * N)):
            cols = pl.ds(ZC + i * 2 * N, 2 * N)
            acc[:, cols] += jnp.dot(t, two_tiles(buf_a, q, 16 + i * 2 * N), preferred_element_type=F32)

    def use_z(q):
        ring_z.shared(q)
        t = tokx[HALO:, columns_of(q)]
        for i in range(ZC // (2 * N)):
            cols = pl.ds(i * 2 * N, 2 * N)
            acc[HALO:, cols] += jnp.dot(t, two_tiles(buf_z, q, i * 2 * N), preferred_element_type=F32)

    use_a(0)

    @pl.loop(1, half - 1)
    def _(k):
        ring_a.step(k)

        @pl.when(k > 1)
        def _():
            use_a(k - 1)
            use_a(chips - k + 1)

    ring_a.at(half - 1)
    ring_z.begin()
    ring_o.begin()
    if half > 2:
        use_a(half - 2)
        use_a(half + 2)
    use_a(half - 1)
    use_a(half + 1)
    ring_a.at(half)
    done_z, done_o = [0], [0]

    def more_z(n=1):
        for _ in range(n):
            if done_z[0] < half:
                done_z[0] += 1
                ring_z.at(done_z[0])

    def more_o(n=1):
        for _ in range(n):
            if done_o[0] < half:
                done_o[0] += 1
                ring_o.at(done_o[0])

    used_z = [-1]

    def use_z_to(k):
        while used_z[0] < min(k, half):
            used_z[0] += 1
            use_z(used_z[0])
            if 0 < used_z[0] < half:
                use_z(chips - used_z[0])

    more_z()
    use_a(half)

    keep = jnp.where(s == 0, 0.0, 1.0)
    act = []
    for t in range(XG // N):
        cols = slice(t * N, (t + 1) * N)
        xbc = acc[:, ZC + t * N : ZC + (t + 1) * N].astype(BF).astype(F32)
        xf[0:HALO, cols] = xbc[0:HALO] * keep
        xf[HALO:, cols] = xbc[HALO:]
        conv = jnp.broadcast_to(cbias_ref[0:1, cols], (BLOCK, N))
        for k in range(KCONV):
            start = HALO - KCONV + 1 + k
            conv = conv + taps_ref[k : k + 1, cols] * xf[start : start + BLOCK, cols]
        act.append(silu(conv))
    xs, bmat, cmat = act[:XT], act[XT], act[XT + 1]

    draw = acc_dt[HALO:, 0:HG].astype(BF).astype(F32) + dtb_ref[0:1, :]
    dt = jnp.maximum(draw, 0.0) + jnp.log1p(jnp.exp(-jnp.abs(draw)))
    rows = lax.broadcasted_iota(jnp.int32, (BLOCK, BLOCK), 0)
    cols = lax.broadcasted_iota(jnp.int32, (BLOCK, BLOCK), 1)
    causal = rows >= cols
    cum = jnp.dot(
        causal.astype(F32), -dt * rate_ref[0:1, :], preferred_element_type=F32, precision=HIGHEST
    )
    cum_rows = jnp.concatenate([cum, jnp.zeros((BLOCK, N - HG), F32)], axis=1).T
    end = cum[BLOCK - 1 : BLOCK]
    tail = jnp.exp(end - cum)
    whole = jnp.exp(end)

    more_z()

    b_turned = bmat.T.astype(BF)
    dosed = [xs[j] * head_lanes(dt, j) for j in range(XT)]
    states = [
        jnp.dot(b_turned, (dosed[j] * head_lanes(tail, j)).astype(BF), preferred_element_type=F32)
        for j in range(XT)
    ]
    fades = [head_lanes(whole, j) for j in range(XT)]
    pair = XT // 2
    first_core = core == 0

    def joined(parts):
        return jnp.concatenate(parts, axis=1)

    low_state, high_state = joined(states[:pair]), joined(states[pair:])
    low_fade, high_fade = joined(fades[:pair]), joined(fades[pair:])
    kept = jnp.where(first_core, low_state, high_state)
    kept_fade = jnp.where(first_core, low_fade, high_fade)
    x1_out[0:N] = jnp.where(first_core, high_state, low_state).astype(BF)
    x1_out[N : N + 16] = two_parts(jnp.where(first_core, high_fade, low_fade))
    swap1 = pltpu.make_async_remote_copy(
        src_ref=x1_out, dst_ref=x1_in, send_sem=x1_send, recv_sem=x1_recv,
        device_id=sib, device_id_type=MESH,
    )
    swap1.start()

    more_z()

    scores = lax.dot_general(
        cmat.astype(BF), bmat.astype(BF), (((1,), (1,)), ((), ())), preferred_element_type=F32
    )
    lane = lax.broadcasted_iota(jnp.int32, (BLOCK, N), 1)

    def inner(j):
        mix = []
        for h in (2 * j, 2 * j + 1):
            gap = jnp.where(causal, cum[:, h : h + 1] - cum_rows[h : h + 1, :], -1e30)
            mix.append((jnp.exp(gap) * scores).astype(BF))
        low = jnp.where(lane < P_SIZE, dosed[j], 0.0).astype(BF)
        high = jnp.where(lane < P_SIZE, 0.0, dosed[j]).astype(BF)
        y = jnp.dot(
            jnp.concatenate(mix, axis=1), jnp.concatenate([low, high], axis=0),
            preferred_element_type=F32,
        )
        return y + head_lanes(skip_ref[0:1, :], j) * xs[j]

    ys = [inner(j) for j in range(pair)]

    swap1.wait_recv()
    other = x1_in[0:N].astype(F32)
    other_fade = one_row(x1_in[N : N + 16])
    state0 = jnp.where(first_core, kept, other)
    state1 = jnp.where(first_core, other, kept)
    fade0 = jnp.where(first_core, kept_fade, other_fade)
    fade1 = jnp.where(first_core, other_fade, kept_fade)
    chip_state = (state0 * fade1 + state1).astype(BF)
    chip_fade = two_parts(fade0 * fade1)
    for o in range(chips):
        i, j = o % half, o // half
        st_out[o, 0:tile_rows] = chip_state[i * tile_rows : (i + 1) * tile_rows, j * N : (j + 1) * N]
        st_out[o, tile_rows : tile_rows + 16] = chip_fade[:, j * N : (j + 1) * N]

    def peer(o):
        return (d, 2 * o + core)

    gather_states = Exchange(st_out, st_in, chips, z, peer, e1_send, e1_recv)
    gather_states.begin()

    more_z()
    more_o()
    ys += [inner(j) for j in range(pair, XT)]
    use_z_to(2)
    more_z()

    gather_states.arrive()
    carry = jnp.zeros((tile_rows, N), F32)
    for q in range(chips):
        hin_out[q] = carry.astype(BF)
        carry = carry * one_row(st_in[q, tile_rows : tile_rows + 16]) + st_in[q, 0:tile_rows].astype(F32)
    return_states = Exchange(hin_out, hin_in, chips, z, peer, e2_send, e2_recv)
    return_states.begin()

    more_o()
    more_z()
    use_z_to(4)

    return_states.arrive()
    entry = joined([hin_in[j * half : (j + 1) * half].reshape(N, N) for j in range(pair)]).astype(F32)
    middle = entry * fade0 + state0
    x2_out[...] = jnp.where(first_core, middle, entry).astype(BF)
    swap2 = pltpu.make_async_remote_copy(
        src_ref=x2_out, dst_ref=hfull.at[core], send_sem=x2_send, recv_sem=x2_recv,
        device_id=sib, device_id_type=MESH,
    )
    swap2.start()
    hfull[core] = jnp.where(first_core, entry, middle).astype(BF)

    more_z()
    use_z_to(6)
    more_o()
    more_z(half)
    use_z_to(half)
    swap2.wait_recv()

    grown = jnp.exp(cum)
    c_half = cmat.astype(BF)
    gated = []
    square = jnp.zeros((BLOCK, 1), F32)
    for j in range(XT):
        h_in = hfull[j // pair, :, (j % pair) * N : (j % pair + 1) * N]
        y = ys[j] + head_lanes(grown, j) * jnp.dot(c_half, h_in, preferred_element_type=F32)
        g = y * silu(acc[HALO:, j * N : (j + 1) * N].astype(BF).astype(F32))
        square = square + jnp.sum(g * g, axis=1, keepdims=True)
        gated.append(g)
    scale = lax.rsqrt(square / ZC + 1e-05)
    for j in range(XT):
        normed[:, j * N : (j + 1) * N] = (gated[j] * scale * gain_ref[0:1, j * N : (j + 1) * N]).astype(BF)

    def send_term(o, q, slot):
        return pltpu.make_async_remote_copy(
            src_ref=t_out.at[q], dst_ref=r_in.at[slot], send_sem=rs_send.at[q], recv_sem=rs_recv.at[slot],
            device_id=(o, s), device_id_type=MESH,
        )

    def term(q):
        ring_o.shared(q)
        w = jnp.concatenate([buf_o[q, 0], buf_o[q, 1]], axis=1)
        value = jnp.dot(normed[...], w, preferred_element_type=F32).astype(BF)
        o = lax.rem(z - q + chips, chips)
        t_out[q] = value

        @pl.when(o != d)
        def _():
            send_term(o, q, d).start()

        @pl.when(o == d)
        def _():
            r_in[d] = value

    for lo, hi in batches(half):
        more_o(hi - done_o[0])
        steps = hi - lo + 1
        count = 2 * hi + 1 if lo == 0 else (2 * (half - lo) + 1 if hi == half else 2 * steps)

        @pl.loop(0, count)
        def _(i):
            at = lax.rem(i + d, count)
            if lo == 0:
                term(lax.rem(at - hi + chips, chips))
            elif hi == half:
                term(lo + at)
            else:
                term(jnp.where(at < steps, lo + at, chips - hi + at - steps))

    total = jnp.zeros((BLOCK, 2 * N), F32)

    @pl.loop(1, n_dp)
    def _(k):
        e = lax.rem(d + k, n_dp)
        send_term(e, e, e).wait_recv()

    for e in range(n_dp):
        total = total + r_in[e].astype(F32)
    out_ref[...] = total.astype(BF)

    @pl.loop(0, chips)
    def _(q):
        o = lax.rem(z - q + chips, chips)

        @pl.when(o != d)
        def _():
            send_term(o, q, d).wait_send()

    halo.wait_send()
    swap1.wait_send()
    swap2.wait_send()
    gather_states.drain()
    return_states.drain()
    ring_a.drain()
    ring_z.drain()
    ring_o.drain()


def per_device(
    tokens, w_in, conv_weight, conv_bias, dt_bias, decay_rate, skip_gain, norm_gain, w_out
):
    chips, n_dp = lax.axis_size("seq") // 2, lax.axis_size("dp")
    rows = HALO + BLOCK
    tile_rows = 2 * N // chips
    dma = pltpu.SemaphoreType.DMA
    vmem = pl.BlockSpec(memory_space=pltpu.VMEM)
    return pl.pallas_call(
        functools.partial(mixer_kernel, chips, n_dp),
        out_shape=jax.ShapeDtypeStruct((BLOCK, 2 * N), BF),
        in_specs=[pl.BlockSpec(memory_space=pl.ANY)] + [vmem] * 8,
        out_specs=vmem,
        scratch_shapes=[
            pltpu.VMEM((rows, tokens.shape[1]), BF),
            pltpu.VMEM((chips, 2, AROWS, N), BF),
            pltpu.VMEM((chips, 2, ZC, N), BF),
            pltpu.VMEM((chips, 2, ZC, N), BF),
            pltpu.VMEM((rows, ZC + XG), F32),
            pltpu.VMEM((rows, 16), F32),
            pltpu.VMEM((rows, XG), F32),
            pltpu.VMEM((N + 16, 2 * N), BF),
            pltpu.VMEM((N + 16, 2 * N), BF),
            pltpu.VMEM((chips, tile_rows + 16, N), BF),
            pltpu.VMEM((chips, tile_rows + 16, N), BF),
            pltpu.VMEM((chips, tile_rows, N), BF),
            pltpu.VMEM((chips, tile_rows, N), BF),
            pltpu.VMEM((N, 2 * N), BF),
            pltpu.VMEM((2, N, 2 * N), BF),
            pltpu.VMEM((BLOCK, ZC), BF),
            pltpu.VMEM((chips, BLOCK, 2 * N), BF),
            pltpu.VMEM((n_dp, BLOCK, 2 * N), BF),
            dma, dma, dma, dma, dma, dma, dma,
            dma((chips,)), dma((chips,)), dma((chips,)), dma((chips,)), dma((chips,)), dma((n_dp,)),
            *ring_sems(chips),
            *ring_sems(chips),
            *ring_sems(chips),
        ],
        compiler_params=pltpu.CompilerParams(
            collective_id=0, has_side_effects=True, vmem_limit_bytes=VMEM_LIMIT
        ),
    )(
        tokens, w_in, conv_weight, conv_bias[None], dt_bias[None], decay_rate[None], skip_gain[None],
        norm_gain[None], w_out,
    )


def solution(mesh):
    placed = (
        P("seq", None),
        P("seq", "dp"),
        P(None, "dp"),
        P("dp"),
        P("dp"),
        P("dp"),
        P("dp"),
        P("dp"),
        P("dp", "seq"),
    )
    return jax.shard_map(
        per_device, mesh=mesh, in_specs=placed, out_specs=P("seq", "dp"), check_vma=False
    )
```

```python
import functools
import math

import jax
import jax.numpy as jnp
from jax import lax
from jax.experimental import pallas as pl
from jax.experimental.pallas import tpu as pltpu
from jax.sharding import PartitionSpec as P

P_SIZE = 64
N = 128
KCONV = 4
BLOCK = 128
HALF = 64
HG = 8
XG = 768
CG = 1288
ZC = 512
HALO = 8
AROWS = 16 + XG
XT = ZC // N
BF = jnp.bfloat16
F32 = jnp.float32
MESH = pl.DeviceIdType.MESH
HIGHEST = lax.Precision.HIGHEST
VMEM_LIMIT = 56 * 1024 * 1024

A_PARTS = ((0, 208), (208, 192), (400, 192), (592, 192))
W_PARTS = ((0, 128), (128, 128), (256, 128), (384, 128))

STAGES = (1, 2, 3, 5)


class Ring:
    def __init__(self, buf, parts, chips, core, right, left, sib, sems):
        self.buf, self.parts, self.chips, self.core = buf, parts, chips, core
        self.right, self.left, self.sib = right, left, sib
        self.recv, self.sent, self.srecv, self.ssent = sems
        self.half = chips // 2
        self.n = len(parts)

    def far(self, h, going_right):
        return (h < self.n // 2) == going_right

    def _hop(self, q, to, step, h, going_right):
        lo, size = self.parts[h]
        way = 0 if going_right else 1
        if isinstance(step, int):
            last = 2 if step == self.half - 1 else 0
        else:
            last = jnp.where(step == self.half - 1, 2, 0)
        return pltpu.make_async_remote_copy(
            src_ref=self.buf.at[q, self.core, pl.ds(lo, size)],
            dst_ref=self.buf.at[to, self.core, pl.ds(lo, size)],
            send_sem=self.sent.at[way + last],
            recv_sem=self.recv.at[step, h],
            device_id=self.right if going_right else self.left,
            device_id_type=MESH,
        )

    def _share(self, q, step):
        return pltpu.make_async_remote_copy(
            src_ref=self.buf.at[q, self.core],
            dst_ref=self.buf.at[q, self.core],
            send_sem=self.ssent,
            recv_sem=self.srecv.at[step],
            device_id=self.sib,
            device_id_type=MESH,
        )

    def _share_part(self, q, step, h):
        lo, size = self.parts[h]
        place = self.buf.at[q, self.core, pl.ds(lo, size)]
        return self._taken(place, self.ssent, self.srecv.at[step])

    def _taken(self, ref, send_sem, recv_sem):
        return pltpu.make_async_remote_copy(
            src_ref=ref, dst_ref=ref, send_sem=send_sem, recv_sem=recv_sem,
            device_id=self.sib, device_id_type=MESH,
        )

    def begin(self):
        for h in range(self.n):
            self._hop(0, 1, 0, h, True).start()
            self._hop(0, self.chips - 1, 0, h, False).start()
        self._share(0, 0).start()

    def step(self, k):
        z = self.chips
        final = isinstance(k, int) and k == self.half
        for h in range(self.n):
            lo, size = self.parts[h]
            places = self.buf.at[pl.ds(0, 1 if final else 2), self.core, pl.ds(lo, size)]
            self._taken(places, self.ssent, self.recv.at[k - 1, h]).wait_recv()
            if final:
                self._share_part(k, k, h).start()
                continue
            right = self._hop(k, k + 1, k, h, True)
            left = self._hop(z - k, z - k - 1, k, h, False)
            far, near = (right, left) if self.far(h, True) else (left, right)
            far.start()
            pl.when(k < self.half - 1)(near.start)
        if not final:
            self._share(k, k).start()
            self._share(z - k, k).start()

    def shared(self, k):
        both = 1 if isinstance(k, int) and k in (0, self.half) else 2
        places = self.buf.at[pl.ds(0, both), self.core]
        self._taken(places, self.ssent, self.srecv.at[k]).wait_recv()

    def drain(self):
        for way in range(2):
            blocks = self.buf.at[pl.ds(0, self.half - 1), self.core]
            self._taken(blocks, self.sent.at[way], self.srecv.at[0]).wait_send()
            hs = [h for h in range(self.n) if self.far(h, way == 0)]
            lo, size = self.parts[hs[0]][0], sum(self.parts[h][1] for h in hs)
            rows = self.buf.at[0, self.core, pl.ds(lo, size)]
            self._taken(rows, self.sent.at[2 + way], self.srecv.at[0]).wait_send()
        self._taken(self.buf.at[:, self.core], self.ssent, self.srecv.at[0]).wait_send()


def ring_sems(chips, parts):
    dma = pltpu.SemaphoreType.DMA
    return [dma((chips // 2, len(parts))), dma((4,)), dma((chips // 2 + 1,)), dma]


class Exchange:
    def __init__(self, out, inn, chips, z, peer, sent, recv):
        self.out, self.inn, self.chips, self.z, self.peer = out, inn, chips, z, peer
        self.sent, self.recv = sent, recv
        half = chips // 2
        self.order = [half] + [k for j in range(1, half) for k in (half - j, half + j)]

    def _copy(self, src, dst, device):
        return pltpu.make_async_remote_copy(
            src_ref=src, dst_ref=dst, send_sem=self.sent, recv_sem=self.recv,
            device_id=device, device_id_type=MESH,
        )

    def begin(self):
        for k in self.order:
            o = lax.rem(self.z + k, self.chips)
            self._copy(self.out.at[o], self.inn.at[self.z], self.peer(o)).start()
        self.inn[self.z] = self.out[self.z]

    def _all(self):
        others = pl.ds(0, self.chips - 1)
        return self._copy(self.out.at[others], self.inn.at[others], self.peer(self.z))

    def arrive(self):
        self._all().wait_recv()

    def drain(self):
        self._all().wait_send()


def silu(v):
    return v / (1.0 + jnp.exp(-v))


def two_parts(row):
    shape = (16, row.shape[1])
    high = row.astype(BF).astype(F32)
    low = row - high
    at = lax.broadcasted_iota(jnp.int32, shape, 0)
    high, low = jnp.broadcast_to(high, shape), jnp.broadcast_to(low, shape)
    return jnp.where(at == 0, high, jnp.where(at == 1, low, 0.0)).astype(BF)


def one_row(tile):
    tile = tile.astype(F32)
    return tile[0:1] + tile[1:2]


def head_lanes(values, j):
    shape = (values.shape[0], N)
    lane = lax.broadcasted_iota(jnp.int32, shape, 1)
    first = jnp.broadcast_to(values[:, 2 * j : 2 * j + 1], shape)
    second = jnp.broadcast_to(values[:, 2 * j + 1 : 2 * j + 2], shape)
    return jnp.where(lane < P_SIZE, first, second)


def mixer_kernel(
    chips, n_dp,
    tok_hbm, win_hbm, taps_hbm, cbias_hbm, dtb_hbm, rate_hbm, skip_hbm, gain_hbm, wout_hbm,
    out_ref,
    taps_ref, cbias_ref, dtb_ref, rate_ref, skip_ref, gain_ref, win_ref,
    tokx, buf_a, buf_z, buf_o, acc, acc_dt, xf, x1_out, x1_in, st_out, st_in, fade_out, fade_in, kept_ref, kept_fade_ref, c_ref, cum_ref, y_ref, hin_out, hin_in,
    x2_out, hfull, normed, t_out, r_in, p_out, p_in,
    local_sem, halo_send, halo_recv, x1_send, x1_recv, x2_send, x2_recv,
    e1_send, e1_recv, f1_send, f1_recv, e2_send, e2_recv, rs_send, rs_recv, *sems,
):
    d, s = lax.axis_index("dp"), lax.axis_index("seq")
    n_seq = 2 * chips
    half = chips // 2
    core, z = lax.rem(s, 2), s // 2
    right = (d, lax.rem(s + 2, n_seq))
    left = (d, lax.rem(s + n_seq - 2, n_seq))
    sib = (d, s + 1 - 2 * core)
    nxt = (d, lax.rem(s + 1, n_seq))
    odd = (d, lax.rem(s + n_seq - 1 + 2 * core, n_seq))
    tile_rows = 2 * N // chips
    side = math.isqrt(n_dp)
    y_at, x_at = d // side, lax.rem(d, side)

    sources = [
        (win_hbm, win_ref), (wout_hbm, buf_o.at[0, core]), (tok_hbm, tokx),
        (taps_hbm, taps_ref), (cbias_hbm, cbias_ref.at[0]),
        (dtb_hbm, dtb_ref), (rate_hbm, rate_ref), (skip_hbm, skip_ref), (gain_hbm, gain_ref),
    ]
    n_first = 2
    local = [
        pltpu.make_async_copy(here, there, local_sem.at[i]) for i, (here, there) in enumerate(sources)
    ]
    first, own, later = local[:n_first], local[n_first], local[n_first + 1 :]
    for copy in local:
        copy.start()

    barrier = pltpu.get_barrier_semaphore()

    def greet(device):
        pl.semaphore_signal(barrier, inc=1, device_id=device, device_id_type=MESH)

    greet(right)
    greet(left)

    @pl.loop(1, side)
    def _(k):
        greet((y_at * side + lax.rem(x_at + k, side), s))
        greet((lax.rem(y_at + k, side) * side + x_at, s))

    greet(sib)
    greet(odd)

    acc[...] = jnp.zeros_like(acc)
    acc_dt[...] = jnp.zeros_like(acc_dt)
    for copy in first:
        copy.wait()
    buf_a[0, core, 0:XG] = win_ref[ZC : ZC + XG]
    last_rows = win_ref[ZC + XG : CG].astype(F32)
    buf_a[0, core, XG:AROWS] = jnp.concatenate([last_rows, jnp.zeros((16 - HG, N), F32)], axis=0).astype(BF)
    buf_z[0, core] = win_ref[0:ZC]
    pl.semaphore_wait(barrier, 2 * side + 2)

    ring_a = Ring(buf_a, A_PARTS, chips, core, right, left, sib, sems[0:4])
    ring_z = Ring(buf_z, W_PARTS, chips, core, right, left, sib, sems[4:8])
    ring_o = Ring(buf_o, W_PARTS, chips, core, right, left, sib, sems[8:12])
    ring_a.begin()
    for copy in later:
        copy.wait()
    own.wait()

    def columns_of(q):
        owner = lax.rem(z - q + chips, chips)
        return pl.ds(pl.multiple_of(owner * 2 * N, 2 * N), 2 * N)

    turned = (((1,), (1,)), ((), ()))

    def both_cores(buf, q, row, size):
        return jnp.concatenate([buf[q, 0, row : row + size], buf[q, 1, row : row + size]], axis=1)

    def use_a(q):
        t = tokx[:, columns_of(q)]
        w = both_cores(buf_a, q, XG, 16)
        acc_dt[...] += lax.dot_general(t, w, turned, preferred_element_type=F32)
        for i in range(XG // (2 * N)):
            w = both_cores(buf_a, q, i * 2 * N, 2 * N)
            acc[:, pl.ds(ZC + i * 2 * N, 2 * N)] += lax.dot_general(t, w, turned, preferred_element_type=F32)

    def use_z(q):
        t = tokx[:, columns_of(q)]
        for i in range(ZC // (2 * N)):
            w = both_cores(buf_z, q, i * 2 * N, 2 * N)
            acc[:, pl.ds(i * 2 * N, 2 * N)] += lax.dot_general(t, w, turned, preferred_element_type=F32)

    def use_both(ring, use, k):
        ring.shared(k)
        use(k)
        if not (isinstance(k, int) and k in (0, half)):
            use(chips - k)

    use_both(ring_a, use_a, 0)

    @pl.loop(1, half)
    def _(k):
        ring_a.step(k)

        @pl.when(k > 1)
        def _():
            use_both(ring_a, use_a, k - 1)

    ring_z.begin()
    ring_o.begin()
    use_both(ring_a, use_a, half - 1)
    ring_a.step(half)
    use_both(ring_z, use_z, 0)
    use_both(ring_a, use_a, half)

    halo = pltpu.make_async_remote_copy(
        src_ref=acc.at[pl.ds(BLOCK - HALO, HALO), pl.ds(ZC, XG)],
        dst_ref=xf.at[pl.ds(0, HALO)],
        send_sem=halo_send,
        recv_sem=halo_recv,
        device_id=nxt,
        device_id_type=MESH,
    )
    halo.start()
    xf[HALO:, :] = acc[:, ZC:].astype(BF).astype(F32)
    halo.wait_recv()

    keep = jnp.where(s == 0, 0.0, 1.0)
    act = []
    for t in range(XG // N):
        cols = slice(t * N, (t + 1) * N)
        xf[0:HALO, cols] = xf[0:HALO, cols].astype(BF).astype(F32) * keep
        conv = jnp.broadcast_to(cbias_ref[0:1, cols], (BLOCK, N))
        for k in range(KCONV):
            start = HALO - KCONV + 1 + k
            conv = conv + taps_ref[k : k + 1, cols] * xf[start : start + BLOCK, cols]
        act.append(silu(conv))
    xs, bmat, cmat = act[:XT], act[XT], act[XT + 1]

    draw = acc_dt[:, 0:HG].astype(BF).astype(F32) + dtb_ref[0:1, :]
    dt = jnp.maximum(draw, 0.0) + jnp.log1p(jnp.exp(-jnp.abs(draw)))
    rows = lax.broadcasted_iota(jnp.int32, (BLOCK, BLOCK), 0)
    cols = lax.broadcasted_iota(jnp.int32, (BLOCK, BLOCK), 1)
    causal = rows >= cols
    cum = jnp.dot(
        causal.astype(F32), -dt * rate_ref[0:1, :], preferred_element_type=F32, precision=HIGHEST
    )
    cum_rows = jnp.concatenate([cum, jnp.zeros((BLOCK, N - HG), F32)], axis=1).T
    end = cum[BLOCK - 1 : BLOCK]
    tail = jnp.exp(end - cum)
    whole = jnp.exp(end)


    b_turned = bmat.T.astype(BF)
    dosed = [xs[j] * head_lanes(dt, j) for j in range(XT)]
    states = [
        jnp.dot(b_turned, (dosed[j] * head_lanes(tail, j)).astype(BF), preferred_element_type=F32)
        for j in range(XT)
    ]
    fades = [head_lanes(whole, j) for j in range(XT)]
    pair = XT // 2
    first_core = core == 0

    def joined(parts):
        return jnp.concatenate(parts, axis=1)

    low_state, high_state = joined(states[:pair]), joined(states[pair:])
    low_fade, high_fade = joined(fades[:pair]), joined(fades[pair:])
    kept_ref[...] = jnp.where(first_core, low_state, high_state)
    kept_fade_ref[...] = jnp.where(first_core, low_fade, high_fade)
    c_ref[...] = cmat.astype(BF)
    cum_ref[...] = cum
    x1_out[0:N] = jnp.where(first_core, high_state, low_state).astype(BF)
    x1_out[N : N + 16] = two_parts(jnp.where(first_core, high_fade, low_fade))
    swap1 = pltpu.make_async_remote_copy(
        src_ref=x1_out, dst_ref=x1_in, send_sem=x1_send, recv_sem=x1_recv,
        device_id=sib, device_id_type=MESH,
    )
    swap1.start()


    scores = lax.dot_general(
        cmat.astype(BF), bmat.astype(BF), (((1,), (1,)), ((), ())), preferred_element_type=F32
    )
    lane = lax.broadcasted_iota(jnp.int32, (BLOCK, N), 1)

    def inner(j):
        mix = []
        for h in (2 * j, 2 * j + 1):
            gap = jnp.where(causal, cum[:, h : h + 1] - cum_rows[h : h + 1, :], -1e30)
            mix.append((jnp.exp(gap) * scores).astype(BF))
        low = jnp.where(lane < P_SIZE, dosed[j], 0.0).astype(BF)
        high = jnp.where(lane < P_SIZE, 0.0, dosed[j]).astype(BF)
        y = jnp.dot(
            jnp.concatenate(mix, axis=1), jnp.concatenate([low, high], axis=0),
            preferred_element_type=F32,
        )
        return y + head_lanes(skip_ref[0:1, :], j) * xs[j]

    for j in range(XT):
        y_ref[:, j * N : (j + 1) * N] = inner(j)

    def peer(o):
        return (d, 2 * o + core)

    gather_fades = Exchange(fade_out, fade_in, chips, z, peer, f1_send, f1_recv)
    gather_states = Exchange(st_out, st_in, chips, z, peer, e1_send, e1_recv)
    return_states = Exchange(hin_out, hin_in, chips, z, peer, e2_send, e2_recv)
    swap2 = pltpu.make_async_remote_copy(
        src_ref=x2_out, dst_ref=hfull.at[core], send_sem=x2_send, recv_sem=x2_recv,
        device_id=sib, device_id_type=MESH,
    )

    def pair_states():
        swap1.wait_recv()
        kept, kept_fade = kept_ref[...], kept_fade_ref[...]
        other = x1_in[0:N].astype(F32)
        other_fade = one_row(x1_in[N : N + 16])
        state0 = jnp.where(first_core, kept, other)
        state1 = jnp.where(first_core, other, kept)
        fade0 = jnp.where(first_core, kept_fade, other_fade)
        fade1 = jnp.where(first_core, other_fade, kept_fade)
        kept_ref[...] = state0
        kept_fade_ref[...] = fade0
        chip_state = (state0 * fade1 + state1).astype(BF)
        chip_fade = fade0 * fade1
        for o in range(chips):
            i, j = o % half, o // half
            st_out[o] = chip_state[i * tile_rows : (i + 1) * tile_rows, j * N : (j + 1) * N]
            fade_out[o] = chip_fade[:, j * N : (j + 1) * N]
        gather_fades.begin()
        gather_states.begin()

    def scan_chips():
        gather_fades.arrive()
        gather_states.arrive()
        carry = jnp.zeros((tile_rows, N), F32)
        for q in range(chips):
            hin_out[q] = carry.astype(BF)
            carry = carry * fade_in[q] + st_in[q].astype(F32)
        return_states.begin()

    def enter():
        return_states.arrive()
        entry = joined([hin_in[j * half : (j + 1) * half].reshape(N, N) for j in range(pair)]).astype(F32)
        middle = entry * kept_fade_ref[...] + kept_ref[...]
        x2_out[...] = jnp.where(first_core, middle, entry).astype(BF)
        swap2.start()
        hfull[core] = jnp.where(first_core, entry, middle).astype(BF)

    def outer():
        swap2.wait_recv()
        grown = jnp.exp(cum_ref[...])
        for j in range(XT):
            h_in = hfull[j // pair, :, (j % pair) * N : (j % pair + 1) * N]
            y_ref[:, j * N : (j + 1) * N] += head_lanes(grown, j) * jnp.dot(
                c_ref[...], h_in, preferred_element_type=F32
            )

    stages = (pair_states, scan_chips, enter, outer)
    places = STAGES if half >= 8 else (1, 1, 1, 1)

    @pl.loop(1, half)
    def _(k):
        ring_z.step(k)
        ring_o.step(k)

        @pl.when(k > 1)
        def _():
            use_both(ring_z, use_z, k - 1)

        for place, stage in zip(places, stages):
            pl.when(k == place)(stage)

    use_both(ring_z, use_z, half - 1)
    ring_z.step(half)
    ring_o.step(half)
    use_both(ring_z, use_z, half)

    gated = []
    square = jnp.zeros((BLOCK, 1), F32)
    for j in range(XT):
        g = y_ref[:, j * N : (j + 1) * N] * silu(acc[:, j * N : (j + 1) * N].astype(BF).astype(F32))
        square = square + jnp.sum(g * g, axis=1, keepdims=True)
        gated.append(g)
    scale = lax.rsqrt(square / ZC + 1e-05)
    for j in range(XT):
        normed[:, j * N : (j + 1) * N] = (gated[j] * scale * gain_ref[0:1, j * N : (j + 1) * N]).astype(BF)

    ring_o.shared(0)
    ring_o.shared(half)

    @pl.loop(1, half)
    def _(k):
        ring_o.shared(k)

    def hand(src, dst, along, place, send_sem, recv_sem):
        there = (y_at * side + place, s) if along == 0 else (place * side + x_at, s)
        return pltpu.make_async_remote_copy(
            src_ref=src, dst_ref=dst, send_sem=send_sem, recv_sem=recv_sem,
            device_id=there, device_id_type=MESH,
        )

    at = (x_at, y_at)

    @pl.loop(0, n_dp)
    def _(i):
        yo, xo = lax.rem(y_at + 1 + i // side, side), lax.rem(x_at + 1 + i, side)
        q = lax.rem(z - (yo * side + xo) + 2 * chips, chips)
        w = jnp.concatenate([buf_o[q, 0], buf_o[q, 1]], axis=1)
        value = jnp.dot(normed[...], w, preferred_element_type=F32).astype(BF)
        for h, (to, index) in enumerate(((xo, yo), (yo, xo))):
            part = value[h * HALF : (h + 1) * HALF]
            t_out[h, to, index] = part

            @pl.when(to != at[h])
            def _():
                hand(
                    t_out.at[h, to, index], r_in.at[h, at[h], index], h, to,
                    rs_send.at[h], rs_recv.at[h],
                ).start()

            @pl.when(to == at[h])
            def _():
                r_in[h, to, index] = part

    few = pl.ds(0, side - 1)
    for h in range(2):
        first_stage = hand(t_out.at[h, few], r_in.at[h, few], h, at[h], rs_send.at[h], rs_recv.at[h])
        first_stage.wait_recv()
        for j in range(1, side + 1):
            to = lax.rem(at[1 - h] + j, side)
            partial = jnp.zeros((HALF, 2 * N), F32)
            for e in range(side):
                partial = partial + r_in[h, e, to].astype(F32)
            p_out[h, to] = partial.astype(BF)
            if j < side:
                hand(
                    p_out.at[h, to], p_in.at[h, at[1 - h]], 1 - h, to, rs_send.at[2 + h], rs_recv.at[2 + h]
                ).start()
            else:
                p_in[h, to] = partial.astype(BF)
    for h in range(2):
        second_stage = hand(
            p_out.at[h, few], p_in.at[h, few], h, at[h], rs_send.at[2 + h], rs_recv.at[2 + h]
        )
        second_stage.wait_recv()
        total = jnp.zeros((HALF, 2 * N), F32)
        for e in range(side):
            total = total + p_in[h, e].astype(F32)
        out_ref[h * HALF : (h + 1) * HALF] = total.astype(BF)
        second_stage.wait_send()
        hand(t_out.at[h, few], r_in.at[h, few], h, at[h], rs_send.at[h], rs_recv.at[h]).wait_send()
    halo.wait_send()
    swap1.wait_send()
    swap2.wait_send()
    gather_fades.drain()
    gather_states.drain()
    return_states.drain()
    ring_a.drain()
    ring_z.drain()
    ring_o.drain()


def per_device(
    tokens, w_in, conv_weight, conv_bias, dt_bias, decay_rate, skip_gain, norm_gain, w_out
):
    chips, n_dp = lax.axis_size("seq") // 2, lax.axis_size("dp")
    tile_rows = 2 * N // chips
    side = math.isqrt(n_dp)
    dma = pltpu.SemaphoreType.DMA
    vmem = pl.BlockSpec(memory_space=pltpu.VMEM)
    return pl.pallas_call(
        functools.partial(mixer_kernel, chips, n_dp),
        out_shape=jax.ShapeDtypeStruct((BLOCK, 2 * N), BF),
        in_specs=[pl.BlockSpec(memory_space=pl.ANY)] * 9,
        out_specs=vmem,
        scratch_shapes=[
            pltpu.VMEM((KCONV, XG), F32),
            pltpu.VMEM((1, XG), F32),
            pltpu.VMEM((1, HG), F32),
            pltpu.VMEM((1, HG), F32),
            pltpu.VMEM((1, HG), F32),
            pltpu.VMEM((1, ZC), F32),
            pltpu.VMEM((CG, N), BF),
            pltpu.VMEM(tokens.shape, BF),
            pltpu.VMEM((chips, 2, AROWS, N), BF),
            pltpu.VMEM((chips, 2, ZC, N), BF),
            pltpu.VMEM((chips, 2, ZC, N), BF),
            pltpu.VMEM((BLOCK, ZC + XG), F32),
            pltpu.VMEM((BLOCK, 16), F32),
            pltpu.VMEM((HALO + BLOCK, XG), F32),
            pltpu.VMEM((N + 16, 2 * N), BF),
            pltpu.VMEM((N + 16, 2 * N), BF),
            pltpu.VMEM((chips, tile_rows, N), BF),
            pltpu.VMEM((chips, tile_rows, N), BF),
            pltpu.VMEM((chips, 1, N), F32),
            pltpu.VMEM((chips, 1, N), F32),
            pltpu.VMEM((N, 2 * N), F32),
            pltpu.VMEM((1, 2 * N), F32),
            pltpu.VMEM((BLOCK, N), BF),
            pltpu.VMEM((BLOCK, HG), F32),
            pltpu.VMEM((BLOCK, ZC), F32),
            pltpu.VMEM((chips, tile_rows, N), BF),
            pltpu.VMEM((chips, tile_rows, N), BF),
            pltpu.VMEM((N, 2 * N), BF),
            pltpu.VMEM((2, N, 2 * N), BF),
            pltpu.VMEM((BLOCK, ZC), BF),
            pltpu.VMEM((2, side, side, HALF, 2 * N), BF),
            pltpu.VMEM((2, side, side, HALF, 2 * N), BF),
            pltpu.VMEM((2, side, HALF, 2 * N), BF),
            pltpu.VMEM((2, side, HALF, 2 * N), BF),
            dma((9,)), dma, dma, dma, dma, dma, dma,
            dma, dma, dma, dma, dma, dma, dma((4,)), dma((4,)),
            *ring_sems(chips, A_PARTS),
            *ring_sems(chips, W_PARTS),
            *ring_sems(chips, W_PARTS),
        ],
        compiler_params=pltpu.CompilerParams(
            collective_id=0, has_side_effects=True, vmem_limit_bytes=VMEM_LIMIT
        ),
    )(
        tokens, w_in.T, conv_weight, conv_bias, dt_bias[None], decay_rate[None], skip_gain[None],
        norm_gain[None], w_out,
    )


def solution(mesh):
    placed = (
        P("seq", None),
        P("seq", "dp"),
        P(None, "dp"),
        P("dp"),
        P("dp"),
        P("dp"),
        P("dp"),
        P("dp"),
        P("dp", "seq"),
    )
    return jax.shard_map(
        per_device, mesh=mesh, in_specs=placed, out_specs=P("seq", "dp"), check_vma=False
    )
```

```python
import functools
import math

import jax
import jax.numpy as jnp
from jax import lax
from jax.experimental import pallas as pl
from jax.experimental.pallas import tpu as pltpu
from jax.sharding import PartitionSpec as P

P_SIZE = 64
N = 128
KCONV = 4
BLOCK = 128
HALF = 64
HG = 8
XG = 768
CG = 1288
ZC = 512
HALO = 8
AROWS = 16 + XG
XT = ZC // N
BF = jnp.bfloat16
F32 = jnp.float32
MESH = pl.DeviceIdType.MESH
HIGHEST = lax.Precision.HIGHEST
VMEM_LIMIT = 56 * 1024 * 1024

A_PARTS = ((0, 208), (208, 192), (400, 192), (592, 192))
W_PARTS = ((0, 128), (128, 128), (256, 128), (384, 128))

STAGES = (1, 2, 3, 5)


class Ring:
    def __init__(self, buf, parts, chips, core, right, left, sib, sems):
        self.buf, self.parts, self.chips, self.core = buf, parts, chips, core
        self.right, self.left, self.sib = right, left, sib
        self.recv, self.sent, self.srecv, self.ssent = sems
        self.half = chips // 2
        self.n = len(parts)

    def far(self, h, going_right):
        return (h < self.n // 2) == going_right

    def _hop(self, q, to, step, h, going_right):
        lo, size = self.parts[h]
        way = 0 if going_right else 1
        if isinstance(step, int):
            last = 2 if step == self.half - 1 else 0
        else:
            last = jnp.where(step == self.half - 1, 2, 0)
        return pltpu.make_async_remote_copy(
            src_ref=self.buf.at[q, self.core, pl.ds(lo, size)],
            dst_ref=self.buf.at[to, self.core, pl.ds(lo, size)],
            send_sem=self.sent.at[way + last],
            recv_sem=self.recv.at[step, h],
            device_id=self.right if going_right else self.left,
            device_id_type=MESH,
        )

    def _share(self, q, step):
        return pltpu.make_async_remote_copy(
            src_ref=self.buf.at[q, self.core],
            dst_ref=self.buf.at[q, self.core],
            send_sem=self.ssent,
            recv_sem=self.srecv.at[step],
            device_id=self.sib,
            device_id_type=MESH,
        )

    def _share_part(self, q, step, h):
        lo, size = self.parts[h]
        place = self.buf.at[q, self.core, pl.ds(lo, size)]
        return self._taken(place, self.ssent, self.srecv.at[step])

    def _taken(self, ref, send_sem, recv_sem):
        return pltpu.make_async_remote_copy(
            src_ref=ref, dst_ref=ref, send_sem=send_sem, recv_sem=recv_sem,
            device_id=self.sib, device_id_type=MESH,
        )

    def begin(self):
        for h in range(self.n):
            self._hop(0, 1, 0, h, True).start()
            self._hop(0, self.chips - 1, 0, h, False).start()
        self._share(0, 0).start()

    def step(self, k):
        z = self.chips
        final = isinstance(k, int) and k == self.half
        for h in range(self.n):
            lo, size = self.parts[h]
            places = self.buf.at[pl.ds(0, 1 if final else 2), self.core, pl.ds(lo, size)]
            self._taken(places, self.ssent, self.recv.at[k - 1, h]).wait_recv()
            if final:
                self._share_part(k, k, h).start()
                continue
            right = self._hop(k, k + 1, k, h, True)
            left = self._hop(z - k, z - k - 1, k, h, False)
            far, near = (right, left) if self.far(h, True) else (left, right)
            far.start()
            pl.when(k < self.half - 1)(near.start)
        if not final:
            self._share(k, k).start()
            self._share(z - k, k).start()

    def shared(self, k):
        both = 1 if isinstance(k, int) and k in (0, self.half) else 2
        places = self.buf.at[pl.ds(0, both), self.core]
        self._taken(places, self.ssent, self.srecv.at[k]).wait_recv()

    def drain(self):
        for way in range(2):
            blocks = self.buf.at[pl.ds(0, self.half - 1), self.core]
            self._taken(blocks, self.sent.at[way], self.srecv.at[0]).wait_send()
            hs = [h for h in range(self.n) if self.far(h, way == 0)]
            lo, size = self.parts[hs[0]][0], sum(self.parts[h][1] for h in hs)
            rows = self.buf.at[0, self.core, pl.ds(lo, size)]
            self._taken(rows, self.sent.at[2 + way], self.srecv.at[0]).wait_send()
        self._taken(self.buf.at[:, self.core], self.ssent, self.srecv.at[0]).wait_send()


def ring_sems(chips, parts):
    dma = pltpu.SemaphoreType.DMA
    return [dma((chips // 2, len(parts))), dma((4,)), dma((chips // 2 + 1,)), dma]


class Exchange:
    def __init__(self, out, inn, chips, z, peer, sent, recv):
        self.out, self.inn, self.chips, self.z, self.peer = out, inn, chips, z, peer
        self.sent, self.recv = sent, recv
        half = chips // 2
        self.order = [half] + [k for j in range(1, half) for k in (half - j, half + j)]

    def _copy(self, src, dst, device):
        return pltpu.make_async_remote_copy(
            src_ref=src, dst_ref=dst, send_sem=self.sent, recv_sem=self.recv,
            device_id=device, device_id_type=MESH,
        )

    def begin(self):
        for k in self.order:
            o = lax.rem(self.z + k, self.chips)
            self._copy(self.out.at[o], self.inn.at[self.z], self.peer(o)).start()
        self.inn[self.z] = self.out[self.z]

    def _all(self):
        others = pl.ds(0, self.chips - 1)
        return self._copy(self.out.at[others], self.inn.at[others], self.peer(self.z))

    def arrive(self):
        self._all().wait_recv()

    def drain(self):
        self._all().wait_send()


def silu(v):
    return v / (1.0 + jnp.exp(-v))


def two_parts(row):
    shape = (16, row.shape[1])
    high = row.astype(BF).astype(F32)
    low = row - high
    at = lax.broadcasted_iota(jnp.int32, shape, 0)
    high, low = jnp.broadcast_to(high, shape), jnp.broadcast_to(low, shape)
    return jnp.where(at == 0, high, jnp.where(at == 1, low, 0.0)).astype(BF)


def one_row(tile):
    tile = tile.astype(F32)
    return tile[0:1] + tile[1:2]


def head_lanes(values, j):
    shape = (values.shape[0], N)
    lane = lax.broadcasted_iota(jnp.int32, shape, 1)
    first = jnp.broadcast_to(values[:, 2 * j : 2 * j + 1], shape)
    second = jnp.broadcast_to(values[:, 2 * j + 1 : 2 * j + 2], shape)
    return jnp.where(lane < P_SIZE, first, second)


def mixer_kernel(
    chips, n_dp,
    tok_hbm, win_hbm, taps_hbm, cbias_hbm, dtb_hbm, rate_hbm, skip_hbm, gain_hbm, wout_hbm,
    out_ref,
    taps_ref, cbias_ref, dtb_ref, rate_ref, skip_ref, gain_ref, win_ref,
    tokx, buf_a, buf_z, buf_o, acc, acc_dt, xf, x1_out, x1_in, st_out, st_in, fade_out, fade_in, kept_ref, kept_fade_ref, c_ref, cum_ref, y_ref, hin_out, hin_in,
    x2_out, hfull, normed, t_out, r_in, p_out, p_in,
    local_sem, halo_send, halo_recv, x1_send, x1_recv, x2_send, x2_recv,
    e1_send, e1_recv, f1_send, f1_recv, e2_send, e2_recv, rs_send, rs_recv, *sems,
):
    d, s = lax.axis_index("dp"), lax.axis_index("seq")
    n_seq = 2 * chips
    half = chips // 2
    core, z = lax.rem(s, 2), s // 2
    right = (d, lax.rem(s + 2, n_seq))
    left = (d, lax.rem(s + n_seq - 2, n_seq))
    sib = (d, s + 1 - 2 * core)
    nxt = (d, lax.rem(s + 1, n_seq))
    odd = (d, lax.rem(s + n_seq - 1 + 2 * core, n_seq))
    tile_rows = 2 * N // chips
    side = math.isqrt(n_dp)
    y_at, x_at = d // side, lax.rem(d, side)

    sources = [
        (win_hbm, win_ref), (wout_hbm, buf_o.at[0, core]), (tok_hbm, tokx),
        (taps_hbm, taps_ref), (cbias_hbm, cbias_ref.at[0]),
        (dtb_hbm, dtb_ref), (rate_hbm, rate_ref), (skip_hbm, skip_ref), (gain_hbm, gain_ref),
    ]
    n_first = 2
    local = [
        pltpu.make_async_copy(here, there, local_sem.at[i]) for i, (here, there) in enumerate(sources)
    ]
    first, own, later = local[:n_first], local[n_first], local[n_first + 1 :]
    for copy in local:
        copy.start()

    barrier = pltpu.get_barrier_semaphore()

    def greet(device):
        pl.semaphore_signal(barrier, inc=1, device_id=device, device_id_type=MESH)

    greet(right)
    greet(left)

    @pl.loop(1, side)
    def _(k):
        greet((y_at * side + lax.rem(x_at + k, side), s))
        greet((lax.rem(y_at + k, side) * side + x_at, s))

    greet(sib)
    greet(odd)

    acc[...] = jnp.zeros_like(acc)
    acc_dt[...] = jnp.zeros_like(acc_dt)
    for copy in first:
        copy.wait()
    buf_a[0, core, 0:XG] = win_ref[ZC : ZC + XG]
    last_rows = win_ref[ZC + XG : CG].astype(F32)
    buf_a[0, core, XG:AROWS] = jnp.concatenate([last_rows, jnp.zeros((16 - HG, N), F32)], axis=0).astype(BF)
    buf_z[0, core] = win_ref[0:ZC]
    pl.semaphore_wait(barrier, 2 * side + 2)

    ring_a = Ring(buf_a, A_PARTS, chips, core, right, left, sib, sems[0:4])
    ring_z = Ring(buf_z, W_PARTS, chips, core, right, left, sib, sems[4:8])
    ring_o = Ring(buf_o, W_PARTS, chips, core, right, left, sib, sems[8:12])
    ring_a.begin()
    for copy in later:
        copy.wait()
    own.wait()

    def columns_of(q):
        owner = lax.rem(z - q + chips, chips)
        return pl.ds(pl.multiple_of(owner * 2 * N, 2 * N), 2 * N)

    turned = (((1,), (1,)), ((), ()))

    def both_cores(buf, q, row, size):
        return jnp.concatenate([buf[q, 0, row : row + size], buf[q, 1, row : row + size]], axis=1)

    def use_a(q):
        t = tokx[:, columns_of(q)]
        w = both_cores(buf_a, q, XG, 16)
        acc_dt[...] += lax.dot_general(t, w, turned, preferred_element_type=F32)
        for i in range(XG // (2 * N)):
            w = both_cores(buf_a, q, i * 2 * N, 2 * N)
            acc[:, pl.ds(ZC + i * 2 * N, 2 * N)] += lax.dot_general(t, w, turned, preferred_element_type=F32)

    def use_z(q):
        t = tokx[:, columns_of(q)]
        for i in range(ZC // (2 * N)):
            w = both_cores(buf_z, q, i * 2 * N, 2 * N)
            acc[:, pl.ds(i * 2 * N, 2 * N)] += lax.dot_general(t, w, turned, preferred_element_type=F32)

    def use_both(ring, use, k):
        ring.shared(k)
        use(k)
        if not (isinstance(k, int) and k in (0, half)):
            use(chips - k)

    use_both(ring_a, use_a, 0)

    @pl.loop(1, half)
    def _(k):
        ring_a.step(k)

        @pl.when(k > 1)
        def _():
            use_both(ring_a, use_a, k - 1)

    ring_z.begin()
    ring_o.begin()
    use_both(ring_a, use_a, half - 1)
    ring_a.step(half)
    use_both(ring_z, use_z, 0)
    use_both(ring_a, use_a, half)

    halo = pltpu.make_async_remote_copy(
        src_ref=acc.at[pl.ds(BLOCK - HALO, HALO), pl.ds(ZC, XG)],
        dst_ref=xf.at[pl.ds(0, HALO)],
        send_sem=halo_send,
        recv_sem=halo_recv,
        device_id=nxt,
        device_id_type=MESH,
    )
    halo.start()
    xf[HALO:, :] = acc[:, ZC:].astype(BF).astype(F32)
    halo.wait_recv()

    keep = jnp.where(s == 0, 0.0, 1.0)
    act = []
    for t in range(XG // N):
        cols = slice(t * N, (t + 1) * N)
        xf[0:HALO, cols] = xf[0:HALO, cols].astype(BF).astype(F32) * keep
        conv = jnp.broadcast_to(cbias_ref[0:1, cols], (BLOCK, N))
        for k in range(KCONV):
            start = HALO - KCONV + 1 + k
            conv = conv + taps_ref[k : k + 1, cols] * xf[start : start + BLOCK, cols]
        act.append(silu(conv))
    xs, bmat, cmat = act[:XT], act[XT], act[XT + 1]

    draw = acc_dt[:, 0:HG].astype(BF).astype(F32) + dtb_ref[0:1, :]
    dt = jnp.maximum(draw, 0.0) + jnp.log1p(jnp.exp(-jnp.abs(draw)))
    rows = lax.broadcasted_iota(jnp.int32, (BLOCK, BLOCK), 0)
    cols = lax.broadcasted_iota(jnp.int32, (BLOCK, BLOCK), 1)
    causal = rows >= cols
    cum = jnp.dot(
        causal.astype(F32), -dt * rate_ref[0:1, :], preferred_element_type=F32, precision=HIGHEST
    )
    cum_rows = jnp.concatenate([cum, jnp.zeros((BLOCK, N - HG), F32)], axis=1).T
    end = cum[BLOCK - 1 : BLOCK]
    tail = jnp.exp(end - cum)
    whole = jnp.exp(end)


    b_turned = bmat.T.astype(BF)
    dosed = [xs[j] * head_lanes(dt, j) for j in range(XT)]
    states = [
        jnp.dot(b_turned, (dosed[j] * head_lanes(tail, j)).astype(BF), preferred_element_type=F32)
        for j in range(XT)
    ]
    fades = [head_lanes(whole, j) for j in range(XT)]
    pair = XT // 2
    first_core = core == 0

    def joined(parts):
        return jnp.concatenate(parts, axis=1)

    low_state, high_state = joined(states[:pair]), joined(states[pair:])
    low_fade, high_fade = joined(fades[:pair]), joined(fades[pair:])
    kept_ref[...] = jnp.where(first_core, low_state, high_state)
    kept_fade_ref[...] = jnp.where(first_core, low_fade, high_fade)
    c_ref[...] = cmat.astype(BF)
    cum_ref[...] = cum
    x1_out[0:N] = jnp.where(first_core, high_state, low_state).astype(BF)
    x1_out[N : N + 16] = two_parts(jnp.where(first_core, high_fade, low_fade))
    swap1 = pltpu.make_async_remote_copy(
        src_ref=x1_out, dst_ref=x1_in, send_sem=x1_send, recv_sem=x1_recv,
        device_id=sib, device_id_type=MESH,
    )
    swap1.start()


    scores = lax.dot_general(
        cmat.astype(BF), bmat.astype(BF), (((1,), (1,)), ((), ())), preferred_element_type=F32
    )
    lane = lax.broadcasted_iota(jnp.int32, (BLOCK, N), 1)

    def inner(j):
        mix = []
        for h in (2 * j, 2 * j + 1):
            gap = jnp.where(causal, cum[:, h : h + 1] - cum_rows[h : h + 1, :], -1e30)
            mix.append((jnp.exp(gap) * scores).astype(BF))
        low = jnp.where(lane < P_SIZE, dosed[j], 0.0).astype(BF)
        high = jnp.where(lane < P_SIZE, 0.0, dosed[j]).astype(BF)
        y = jnp.dot(
            jnp.concatenate(mix, axis=1), jnp.concatenate([low, high], axis=0),
            preferred_element_type=F32,
        )
        return y + head_lanes(skip_ref[0:1, :], j) * xs[j]

    for j in range(XT):
        y_ref[:, j * N : (j + 1) * N] = inner(j)

    def peer(o):
        return (d, 2 * o + core)

    gather_fades = Exchange(fade_out, fade_in, chips, z, peer, f1_send, f1_recv)
    gather_states = Exchange(st_out, st_in, chips, z, peer, e1_send, e1_recv)
    return_states = Exchange(hin_out, hin_in, chips, z, peer, e2_send, e2_recv)
    swap2 = pltpu.make_async_remote_copy(
        src_ref=x2_out, dst_ref=hfull.at[core], send_sem=x2_send, recv_sem=x2_recv,
        device_id=sib, device_id_type=MESH,
    )

    def pair_states():
        swap1.wait_recv()
        kept, kept_fade = kept_ref[...], kept_fade_ref[...]
        other = x1_in[0:N].astype(F32)
        other_fade = one_row(x1_in[N : N + 16])
        state0 = jnp.where(first_core, kept, other)
        state1 = jnp.where(first_core, other, kept)
        fade0 = jnp.where(first_core, kept_fade, other_fade)
        fade1 = jnp.where(first_core, other_fade, kept_fade)
        kept_ref[...] = state0
        kept_fade_ref[...] = fade0
        chip_state = (state0 * fade1 + state1).astype(BF)
        chip_fade = fade0 * fade1
        for o in range(chips):
            i, j = o % half, o // half
            st_out[o] = chip_state[i * tile_rows : (i + 1) * tile_rows, j * N : (j + 1) * N]
            fade_out[o] = chip_fade[:, j * N : (j + 1) * N]
        gather_fades.begin()
        gather_states.begin()

    def scan_chips():
        gather_fades.arrive()
        gather_states.arrive()
        carry = jnp.zeros((tile_rows, N), F32)
        for q in range(chips):
            hin_out[q] = carry.astype(BF)
            carry = carry * fade_in[q] + st_in[q].astype(F32)
        return_states.begin()

    def enter():
        return_states.arrive()
        entry = joined([hin_in[j * half : (j + 1) * half].reshape(N, N) for j in range(pair)]).astype(F32)
        middle = entry * kept_fade_ref[...] + kept_ref[...]
        x2_out[...] = jnp.where(first_core, middle, entry).astype(BF)
        swap2.start()
        hfull[core] = jnp.where(first_core, entry, middle).astype(BF)

    def outer():
        swap2.wait_recv()
        grown = jnp.exp(cum_ref[...])
        for j in range(XT):
            h_in = hfull[j // pair, :, (j % pair) * N : (j % pair + 1) * N]
            y_ref[:, j * N : (j + 1) * N] += head_lanes(grown, j) * jnp.dot(
                c_ref[...], h_in, preferred_element_type=F32
            )

    stages = (pair_states, scan_chips, enter, outer)
    places = STAGES if half >= 8 else (1, 1, 1, 1)

    @pl.loop(1, half)
    def _(k):
        ring_z.step(k)

        @pl.when(k > 1)
        def _():
            ring_o.step(k - 1)
            use_both(ring_z, use_z, k - 1)

        for place, stage in zip(places, stages):
            pl.when(k == place)(stage)

    use_both(ring_z, use_z, half - 1)
    ring_z.step(half)
    ring_o.step(jnp.int32(half - 1))
    use_both(ring_z, use_z, half)

    gated = []
    square = jnp.zeros((BLOCK, 1), F32)
    for j in range(XT):
        g = y_ref[:, j * N : (j + 1) * N] * silu(acc[:, j * N : (j + 1) * N].astype(BF).astype(F32))
        square = square + jnp.sum(g * g, axis=1, keepdims=True)
        gated.append(g)
    scale = lax.rsqrt(square / ZC + 1e-05)
    for j in range(XT):
        normed[:, j * N : (j + 1) * N] = (gated[j] * scale * gain_ref[0:1, j * N : (j + 1) * N]).astype(BF)

    ring_o.shared(0)

    @pl.loop(1, half - 1)
    def _(k):
        ring_o.shared(k)

    def hand(src, dst, along, place, send_sem, recv_sem):
        there = (y_at * side + place, s) if along == 0 else (place * side + x_at, s)
        return pltpu.make_async_remote_copy(
            src_ref=src, dst_ref=dst, send_sem=send_sem, recv_sem=recv_sem,
            device_id=there, device_id_type=MESH,
        )

    at = (x_at, y_at)

    def term(yo, xo, q):
        w = jnp.concatenate([buf_o[q, 0], buf_o[q, 1]], axis=1)
        value = jnp.dot(normed[...], w, preferred_element_type=F32).astype(BF)
        for h, (to, index) in enumerate(((xo, yo), (yo, xo))):
            part = value[h * HALF : (h + 1) * HALF]
            t_out[h, to, index] = part

            @pl.when(to != at[h])
            def _():
                hand(
                    t_out.at[h, to, index], r_in.at[h, at[h], index], h, to,
                    rs_send.at[h], rs_recv.at[h],
                ).start()

            @pl.when(to == at[h])
            def _():
                r_in[h, to, index] = part

    def terms(of_last_steps):
        @pl.loop(0, n_dp)
        def _(i):
            yo, xo = lax.rem(y_at + 1 + i // side, side), lax.rem(x_at + 1 + i, side)
            q = lax.rem(z - (yo * side + xo) + 2 * chips, chips)
            late = (q >= half - 1) & (q <= half + 1)

            @pl.when(late if of_last_steps else ~late)
            def _():
                term(yo, xo, q)

    terms(False)
    ring_o.step(half)
    ring_o.shared(half - 1)
    ring_o.shared(half)
    terms(True)

    few = pl.ds(0, side - 1)
    for h in range(2):
        first_stage = hand(t_out.at[h, few], r_in.at[h, few], h, at[h], rs_send.at[h], rs_recv.at[h])
        first_stage.wait_recv()
        for j in range(1, side + 1):
            to = lax.rem(at[1 - h] + j, side)
            partial = jnp.zeros((HALF, 2 * N), F32)
            for e in range(side):
                partial = partial + r_in[h, e, to].astype(F32)
            p_out[h, to] = partial.astype(BF)
            if j < side:
                hand(
                    p_out.at[h, to], p_in.at[h, at[1 - h]], 1 - h, to, rs_send.at[2 + h], rs_recv.at[2 + h]
                ).start()
            else:
                p_in[h, to] = partial.astype(BF)
    for h in range(2):
        second_stage = hand(
            p_out.at[h, few], p_in.at[h, few], h, at[h], rs_send.at[2 + h], rs_recv.at[2 + h]
        )
        second_stage.wait_recv()
        total = jnp.zeros((HALF, 2 * N), F32)
        for e in range(side):
            total = total + p_in[h, e].astype(F32)
        out_ref[h * HALF : (h + 1) * HALF] = total.astype(BF)
        second_stage.wait_send()
        hand(t_out.at[h, few], r_in.at[h, few], h, at[h], rs_send.at[h], rs_recv.at[h]).wait_send()
    halo.wait_send()
    swap1.wait_send()
    swap2.wait_send()
    gather_fades.drain()
    gather_states.drain()
    return_states.drain()
    ring_a.drain()
    ring_z.drain()
    ring_o.drain()


def per_device(
    tokens, w_in, conv_weight, conv_bias, dt_bias, decay_rate, skip_gain, norm_gain, w_out
):
    chips, n_dp = lax.axis_size("seq") // 2, lax.axis_size("dp")
    tile_rows = 2 * N // chips
    side = math.isqrt(n_dp)
    dma = pltpu.SemaphoreType.DMA
    vmem = pl.BlockSpec(memory_space=pltpu.VMEM)
    return pl.pallas_call(
        functools.partial(mixer_kernel, chips, n_dp),
        out_shape=jax.ShapeDtypeStruct((BLOCK, 2 * N), BF),
        in_specs=[pl.BlockSpec(memory_space=pl.ANY)] * 9,
        out_specs=vmem,
        scratch_shapes=[
            pltpu.VMEM((KCONV, XG), F32),
            pltpu.VMEM((1, XG), F32),
            pltpu.VMEM((1, HG), F32),
            pltpu.VMEM((1, HG), F32),
            pltpu.VMEM((1, HG), F32),
            pltpu.VMEM((1, ZC), F32),
            pltpu.VMEM((CG, N), BF),
            pltpu.VMEM(tokens.shape, BF),
            pltpu.VMEM((chips, 2, AROWS, N), BF),
            pltpu.VMEM((chips, 2, ZC, N), BF),
            pltpu.VMEM((chips, 2, ZC, N), BF),
            pltpu.VMEM((BLOCK, ZC + XG), F32),
            pltpu.VMEM((BLOCK, 16), F32),
            pltpu.VMEM((HALO + BLOCK, XG), F32),
            pltpu.VMEM((N + 16, 2 * N), BF),
            pltpu.VMEM((N + 16, 2 * N), BF),
            pltpu.VMEM((chips, tile_rows, N), BF),
            pltpu.VMEM((chips, tile_rows, N), BF),
            pltpu.VMEM((chips, 1, N), F32),
            pltpu.VMEM((chips, 1, N), F32),
            pltpu.VMEM((N, 2 * N), F32),
            pltpu.VMEM((1, 2 * N), F32),
            pltpu.VMEM((BLOCK, N), BF),
            pltpu.VMEM((BLOCK, HG), F32),
            pltpu.VMEM((BLOCK, ZC), F32),
            pltpu.VMEM((chips, tile_rows, N), BF),
            pltpu.VMEM((chips, tile_rows, N), BF),
            pltpu.VMEM((N, 2 * N), BF),
            pltpu.VMEM((2, N, 2 * N), BF),
            pltpu.VMEM((BLOCK, ZC), BF),
            pltpu.VMEM((2, side, side, HALF, 2 * N), BF),
            pltpu.VMEM((2, side, side, HALF, 2 * N), BF),
            pltpu.VMEM((2, side, HALF, 2 * N), BF),
            pltpu.VMEM((2, side, HALF, 2 * N), BF),
            dma((9,)), dma, dma, dma, dma, dma, dma,
            dma, dma, dma, dma, dma, dma, dma((4,)), dma((4,)),
            *ring_sems(chips, A_PARTS),
            *ring_sems(chips, W_PARTS),
            *ring_sems(chips, W_PARTS),
        ],
        compiler_params=pltpu.CompilerParams(
            collective_id=0, has_side_effects=True, vmem_limit_bytes=VMEM_LIMIT
        ),
    )(
        tokens, w_in.T, conv_weight, conv_bias, dt_bias[None], decay_rate[None], skip_gain[None],
        norm_gain[None], w_out,
    )


def solution(mesh):
    placed = (
        P("seq", None),
        P("seq", "dp"),
        P(None, "dp"),
        P("dp"),
        P("dp"),
        P("dp"),
        P("dp"),
        P("dp"),
        P("dp", "seq"),
    )
    return jax.shard_map(
        per_device, mesh=mesh, in_specs=placed, out_specs=P("seq", "dp"), check_vma=False
    )
```

```python
import functools
import math

import jax
import jax.numpy as jnp
from jax import lax
from jax.experimental import pallas as pl
from jax.experimental.pallas import tpu as pltpu
from jax.sharding import PartitionSpec as P

P_SIZE = 64
N = 128
KCONV = 4
BLOCK = 128
HALF = 64
HG = 8
XG = 768
CG = 1288
ZC = 512
HALO = 8
AROWS = 16 + XG
XT = ZC // N
BF = jnp.bfloat16
F32 = jnp.float32
MESH = pl.DeviceIdType.MESH
HIGHEST = lax.Precision.HIGHEST
VMEM_LIMIT = 56 * 1024 * 1024

A_PARTS = ((0, 112), (112, 96), (208, 96), (304, 96), (400, 96), (496, 96), (592, 96), (688, 96))
W_PARTS = ((0, 128), (128, 128), (256, 128), (384, 128))

STAGES = (1, 2, 3, 5)


class Ring:
    def __init__(self, buf, parts, chips, core, right, left, sib, sems):
        self.buf, self.parts, self.chips, self.core = buf, parts, chips, core
        self.right, self.left, self.sib = right, left, sib
        self.recv, self.sent, self.srecv, self.ssent = sems
        self.half = chips // 2
        self.n = len(parts)

    def far(self, h, going_right):
        return (h < self.n // 2) == going_right

    def _hop(self, q, to, step, h, going_right):
        lo, size = self.parts[h]
        way = 0 if going_right else 1
        if isinstance(step, int):
            last = 2 if step == self.half - 1 else 0
        else:
            last = jnp.where(step == self.half - 1, 2, 0)
        return pltpu.make_async_remote_copy(
            src_ref=self.buf.at[q, self.core, pl.ds(lo, size)],
            dst_ref=self.buf.at[to, self.core, pl.ds(lo, size)],
            send_sem=self.sent.at[way + last],
            recv_sem=self.recv.at[step, h],
            device_id=self.right if going_right else self.left,
            device_id_type=MESH,
        )

    def _share(self, q, step):
        return pltpu.make_async_remote_copy(
            src_ref=self.buf.at[q, self.core],
            dst_ref=self.buf.at[q, self.core],
            send_sem=self.ssent,
            recv_sem=self.srecv.at[step],
            device_id=self.sib,
            device_id_type=MESH,
        )

    def _share_part(self, q, step, h):
        lo, size = self.parts[h]
        place = self.buf.at[q, self.core, pl.ds(lo, size)]
        return self._taken(place, self.ssent, self.srecv.at[step])

    def _taken(self, ref, send_sem, recv_sem):
        return pltpu.make_async_remote_copy(
            src_ref=ref, dst_ref=ref, send_sem=send_sem, recv_sem=recv_sem,
            device_id=self.sib, device_id_type=MESH,
        )

    def begin(self):
        for h in range(self.n):
            self._hop(0, 1, 0, h, True).start()
            self._hop(0, self.chips - 1, 0, h, False).start()
        self._share(0, 0).start()

    def step(self, k):
        z = self.chips
        final = isinstance(k, int) and k == self.half
        for h in range(self.n):
            lo, size = self.parts[h]
            places = self.buf.at[pl.ds(0, 1 if final else 2), self.core, pl.ds(lo, size)]
            self._taken(places, self.ssent, self.recv.at[k - 1, h]).wait_recv()
            if final:
                self._share_part(k, k, h).start()
                continue
            right = self._hop(k, k + 1, k, h, True)
            left = self._hop(z - k, z - k - 1, k, h, False)
            far, near = (right, left) if self.far(h, True) else (left, right)
            far.start()
            pl.when(k < self.half - 1)(near.start)
        if not final:
            self._share(k, k).start()
            self._share(z - k, k).start()

    def shared(self, k):
        both = 1 if isinstance(k, int) and k in (0, self.half) else 2
        places = self.buf.at[pl.ds(0, both), self.core]
        self._taken(places, self.ssent, self.srecv.at[k]).wait_recv()

    def drain(self):
        for way in range(2):
            blocks = self.buf.at[pl.ds(0, self.half - 1), self.core]
            self._taken(blocks, self.sent.at[way], self.srecv.at[0]).wait_send()
            hs = [h for h in range(self.n) if self.far(h, way == 0)]
            lo, size = self.parts[hs[0]][0], sum(self.parts[h][1] for h in hs)
            rows = self.buf.at[0, self.core, pl.ds(lo, size)]
            self._taken(rows, self.sent.at[2 + way], self.srecv.at[0]).wait_send()
        self._taken(self.buf.at[:, self.core], self.ssent, self.srecv.at[0]).wait_send()


def ring_sems(chips, parts):
    dma = pltpu.SemaphoreType.DMA
    return [dma((chips // 2, len(parts))), dma((4,)), dma((chips // 2 + 1,)), dma]


class Exchange:
    def __init__(self, out, inn, chips, z, peer, sent, recv):
        self.out, self.inn, self.chips, self.z, self.peer = out, inn, chips, z, peer
        self.sent, self.recv = sent, recv
        half = chips // 2
        self.order = [half] + [k for j in range(1, half) for k in (half - j, half + j)]

    def _copy(self, src, dst, device):
        return pltpu.make_async_remote_copy(
            src_ref=src, dst_ref=dst, send_sem=self.sent, recv_sem=self.recv,
            device_id=device, device_id_type=MESH,
        )

    def begin(self):
        for k in self.order:
            o = lax.rem(self.z + k, self.chips)
            self._copy(self.out.at[o], self.inn.at[self.z], self.peer(o)).start()
        self.inn[self.z] = self.out[self.z]

    def _all(self):
        others = pl.ds(0, self.chips - 1)
        return self._copy(self.out.at[others], self.inn.at[others], self.peer(self.z))

    def arrive(self):
        self._all().wait_recv()

    def drain(self):
        self._all().wait_send()


def silu(v):
    return v / (1.0 + jnp.exp(-v))


def two_parts(row):
    shape = (16, row.shape[1])
    high = row.astype(BF).astype(F32)
    low = row - high
    at = lax.broadcasted_iota(jnp.int32, shape, 0)
    high, low = jnp.broadcast_to(high, shape), jnp.broadcast_to(low, shape)
    return jnp.where(at == 0, high, jnp.where(at == 1, low, 0.0)).astype(BF)


def one_row(tile):
    tile = tile.astype(F32)
    return tile[0:1] + tile[1:2]


def head_lanes(values, j):
    shape = (values.shape[0], N)
    lane = lax.broadcasted_iota(jnp.int32, shape, 1)
    first = jnp.broadcast_to(values[:, 2 * j : 2 * j + 1], shape)
    second = jnp.broadcast_to(values[:, 2 * j + 1 : 2 * j + 2], shape)
    return jnp.where(lane < P_SIZE, first, second)


def mixer_kernel(
    chips, n_dp,
    tok_hbm, win_ref, taps_hbm, cbias_hbm, dtb_hbm, rate_hbm, skip_hbm, gain_hbm, wout_hbm,
    out_ref,
    taps_ref, cbias_ref, dtb_ref, rate_ref, skip_ref, gain_ref,
    tokx, buf_a, buf_z, buf_o, acc, acc_dt, xf, x1_out, x1_in, st_out, st_in, fade_out, fade_in, kept_ref, kept_fade_ref, c_ref, cum_ref, y_ref, hin_out, hin_in,
    x2_out, hfull, normed, t_out, r_in, p_out, p_in,
    local_sem, halo_send, halo_recv, x1_send, x1_recv, x2_send, x2_recv,
    e1_send, e1_recv, f1_send, f1_recv, e2_send, e2_recv, rs_send, rs_recv, *sems,
):
    d, s = lax.axis_index("dp"), lax.axis_index("seq")
    n_seq = 2 * chips
    half = chips // 2
    core, z = lax.rem(s, 2), s // 2
    right = (d, lax.rem(s + 2, n_seq))
    left = (d, lax.rem(s + n_seq - 2, n_seq))
    sib = (d, s + 1 - 2 * core)
    nxt = (d, lax.rem(s + 1, n_seq))
    odd = (d, lax.rem(s + n_seq - 1 + 2 * core, n_seq))
    tile_rows = 2 * N // chips
    side = math.isqrt(n_dp)
    y_at, x_at = d // side, lax.rem(d, side)

    sources = [
        (wout_hbm, buf_o.at[0, core]), (tok_hbm, tokx),
        (taps_hbm, taps_ref), (cbias_hbm, cbias_ref.at[0]),
        (dtb_hbm, dtb_ref), (rate_hbm, rate_ref), (skip_hbm, skip_ref), (gain_hbm, gain_ref),
    ]
    n_first = 1
    local = [
        pltpu.make_async_copy(here, there, local_sem.at[i]) for i, (here, there) in enumerate(sources)
    ]
    first, own, later = local[:n_first], local[n_first], local[n_first + 1 :]
    for copy in local:
        copy.start()

    barrier = pltpu.get_barrier_semaphore()

    def greet(device):
        pl.semaphore_signal(barrier, inc=1, device_id=device, device_id_type=MESH)

    greet(right)
    greet(left)

    @pl.loop(1, side)
    def _(k):
        greet((y_at * side + lax.rem(x_at + k, side), s))
        greet((lax.rem(y_at + k, side) * side + x_at, s))

    greet(sib)
    greet(odd)

    acc[...] = jnp.zeros_like(acc)
    acc_dt[...] = jnp.zeros_like(acc_dt)
    for copy in first:
        copy.wait()
    buf_a[0, core, 0:XG] = win_ref[ZC : ZC + XG]
    last_rows = win_ref[ZC + XG : CG].astype(F32)
    buf_a[0, core, XG:AROWS] = jnp.concatenate([last_rows, jnp.zeros((16 - HG, N), F32)], axis=0).astype(BF)
    buf_z[0, core] = win_ref[0:ZC]
    pl.semaphore_wait(barrier, 2 * side + 2)

    ring_a = Ring(buf_a, A_PARTS, chips, core, right, left, sib, sems[0:4])
    ring_z = Ring(buf_z, W_PARTS, chips, core, right, left, sib, sems[4:8])
    ring_o = Ring(buf_o, W_PARTS, chips, core, right, left, sib, sems[8:12])
    ring_a.begin()
    for copy in later:
        copy.wait()
    own.wait()

    def columns_of(q):
        owner = lax.rem(z - q + chips, chips)
        return pl.ds(pl.multiple_of(owner * 2 * N, 2 * N), 2 * N)

    turned = (((1,), (1,)), ((), ()))

    def both_cores(buf, q, row, size):
        return jnp.concatenate([buf[q, 0, row : row + size], buf[q, 1, row : row + size]], axis=1)

    def use_a(q):
        t = tokx[:, columns_of(q)]
        w = both_cores(buf_a, q, XG, 16)
        acc_dt[...] += lax.dot_general(t, w, turned, preferred_element_type=F32)
        for i in range(XG // (2 * N)):
            w = both_cores(buf_a, q, i * 2 * N, 2 * N)
            acc[:, pl.ds(ZC + i * 2 * N, 2 * N)] += lax.dot_general(t, w, turned, preferred_element_type=F32)

    def use_z(q):
        t = tokx[:, columns_of(q)]
        for i in range(ZC // (2 * N)):
            w = both_cores(buf_z, q, i * 2 * N, 2 * N)
            acc[:, pl.ds(i * 2 * N, 2 * N)] += lax.dot_general(t, w, turned, preferred_element_type=F32)

    def use_both(ring, use, k):
        ring.shared(k)
        use(k)
        if not (isinstance(k, int) and k in (0, half)):
            use(chips - k)

    use_both(ring_a, use_a, 0)

    @pl.loop(1, half)
    def _(k):
        ring_a.step(k)

        @pl.when(k > 1)
        def _():
            use_both(ring_a, use_a, k - 1)

    ring_z.begin()
    ring_o.begin()
    use_both(ring_a, use_a, half - 1)
    ring_a.step(half)
    use_both(ring_z, use_z, 0)
    use_both(ring_a, use_a, half)

    halo = pltpu.make_async_remote_copy(
        src_ref=acc.at[pl.ds(BLOCK - HALO, HALO), pl.ds(ZC, XG)],
        dst_ref=xf.at[pl.ds(0, HALO)],
        send_sem=halo_send,
        recv_sem=halo_recv,
        device_id=nxt,
        device_id_type=MESH,
    )
    halo.start()
    xf[HALO:, :] = acc[:, ZC:].astype(BF).astype(F32)
    halo.wait_recv()

    keep = jnp.where(s == 0, 0.0, 1.0)
    act = []
    for t in range(XG // N):
        cols = slice(t * N, (t + 1) * N)
        xf[0:HALO, cols] = xf[0:HALO, cols].astype(BF).astype(F32) * keep
        conv = jnp.broadcast_to(cbias_ref[0:1, cols], (BLOCK, N))
        for k in range(KCONV):
            start = HALO - KCONV + 1 + k
            conv = conv + taps_ref[k : k + 1, cols] * xf[start : start + BLOCK, cols]
        act.append(silu(conv))
    xs, bmat, cmat = act[:XT], act[XT], act[XT + 1]

    draw = acc_dt[:, 0:HG].astype(BF).astype(F32) + dtb_ref[0:1, :]
    dt = jnp.maximum(draw, 0.0) + jnp.log1p(jnp.exp(-jnp.abs(draw)))
    rows = lax.broadcasted_iota(jnp.int32, (BLOCK, BLOCK), 0)
    cols = lax.broadcasted_iota(jnp.int32, (BLOCK, BLOCK), 1)
    causal = rows >= cols
    cum = jnp.dot(
        causal.astype(F32), -dt * rate_ref[0:1, :], preferred_element_type=F32, precision=HIGHEST
    )
    cum_rows = jnp.concatenate([cum, jnp.zeros((BLOCK, N - HG), F32)], axis=1).T
    end = cum[BLOCK - 1 : BLOCK]
    tail = jnp.exp(end - cum)
    whole = jnp.exp(end)


    b_turned = bmat.T.astype(BF)
    dosed = [xs[j] * head_lanes(dt, j) for j in range(XT)]
    states = [
        jnp.dot(b_turned, (dosed[j] * head_lanes(tail, j)).astype(BF), preferred_element_type=F32)
        for j in range(XT)
    ]
    fades = [head_lanes(whole, j) for j in range(XT)]
    pair = XT // 2
    first_core = core == 0

    def joined(parts):
        return jnp.concatenate(parts, axis=1)

    low_state, high_state = joined(states[:pair]), joined(states[pair:])
    low_fade, high_fade = joined(fades[:pair]), joined(fades[pair:])
    kept_ref[...] = jnp.where(first_core, low_state, high_state)
    kept_fade_ref[...] = jnp.where(first_core, low_fade, high_fade)
    c_ref[...] = cmat.astype(BF)
    cum_ref[...] = cum
    x1_out[0:N] = jnp.where(first_core, high_state, low_state).astype(BF)
    x1_out[N : N + 16] = two_parts(jnp.where(first_core, high_fade, low_fade))
    swap1 = pltpu.make_async_remote_copy(
        src_ref=x1_out, dst_ref=x1_in, send_sem=x1_send, recv_sem=x1_recv,
        device_id=sib, device_id_type=MESH,
    )
    swap1.start()


    scores = lax.dot_general(
        cmat.astype(BF), bmat.astype(BF), (((1,), (1,)), ((), ())), preferred_element_type=F32
    )
    lane = lax.broadcasted_iota(jnp.int32, (BLOCK, N), 1)

    def inner(j):
        mix = []
        for h in (2 * j, 2 * j + 1):
            gap = jnp.where(causal, cum[:, h : h + 1] - cum_rows[h : h + 1, :], -1e30)
            mix.append((jnp.exp(gap) * scores).astype(BF))
        low = jnp.where(lane < P_SIZE, dosed[j], 0.0).astype(BF)
        high = jnp.where(lane < P_SIZE, 0.0, dosed[j]).astype(BF)
        y = jnp.dot(
            jnp.concatenate(mix, axis=1), jnp.concatenate([low, high], axis=0),
            preferred_element_type=F32,
        )
        return y + head_lanes(skip_ref[0:1, :], j) * xs[j]

    for j in range(XT):
        y_ref[:, j * N : (j + 1) * N] = inner(j)

    def peer(o):
        return (d, 2 * o + core)

    gather_fades = Exchange(fade_out, fade_in, chips, z, peer, f1_send, f1_recv)
    gather_states = Exchange(st_out, st_in, chips, z, peer, e1_send, e1_recv)
    return_states = Exchange(hin_out, hin_in, chips, z, peer, e2_send, e2_recv)
    swap2 = pltpu.make_async_remote_copy(
        src_ref=x2_out, dst_ref=hfull.at[core], send_sem=x2_send, recv_sem=x2_recv,
        device_id=sib, device_id_type=MESH,
    )

    def pair_states():
        swap1.wait_recv()
        kept, kept_fade = kept_ref[...], kept_fade_ref[...]
        other = x1_in[0:N].astype(F32)
        other_fade = one_row(x1_in[N : N + 16])
        state0 = jnp.where(first_core, kept, other)
        state1 = jnp.where(first_core, other, kept)
        fade0 = jnp.where(first_core, kept_fade, other_fade)
        fade1 = jnp.where(first_core, other_fade, kept_fade)
        kept_ref[...] = state0
        kept_fade_ref[...] = fade0
        chip_state = (state0 * fade1 + state1).astype(BF)
        chip_fade = fade0 * fade1
        for o in range(chips):
            i, j = o % half, o // half
            st_out[o] = chip_state[i * tile_rows : (i + 1) * tile_rows, j * N : (j + 1) * N]
            fade_out[o] = chip_fade[:, j * N : (j + 1) * N]
        gather_fades.begin()
        gather_states.begin()

    def scan_chips():
        gather_fades.arrive()
        gather_states.arrive()
        carry = jnp.zeros((tile_rows, N), F32)
        for q in range(chips):
            hin_out[q] = carry.astype(BF)
            carry = carry * fade_in[q] + st_in[q].astype(F32)
        return_states.begin()

    def enter():
        return_states.arrive()
        entry = joined([hin_in[j * half : (j + 1) * half].reshape(N, N) for j in range(pair)]).astype(F32)
        middle = entry * kept_fade_ref[...] + kept_ref[...]
        x2_out[...] = jnp.where(first_core, middle, entry).astype(BF)
        swap2.start()
        hfull[core] = jnp.where(first_core, entry, middle).astype(BF)

    def outer():
        swap2.wait_recv()
        grown = jnp.exp(cum_ref[...])
        for j in range(XT):
            h_in = hfull[j // pair, :, (j % pair) * N : (j % pair + 1) * N]
            y_ref[:, j * N : (j + 1) * N] += head_lanes(grown, j) * jnp.dot(
                c_ref[...], h_in, preferred_element_type=F32
            )

    stages = (pair_states, scan_chips, enter, outer)
    places = STAGES if half >= 8 else (1, 1, 1, 1)

    @pl.loop(1, half)
    def _(k):
        ring_z.step(k)

        @pl.when(k > 1)
        def _():
            ring_o.step(k - 1)
            use_both(ring_z, use_z, k - 1)

        for place, stage in zip(places, stages):
            pl.when(k == place)(stage)

    use_both(ring_z, use_z, half - 1)
    ring_z.step(half)
    ring_o.step(jnp.int32(half - 1))
    use_both(ring_z, use_z, half)

    gated = []
    square = jnp.zeros((BLOCK, 1), F32)
    for j in range(XT):
        g = y_ref[:, j * N : (j + 1) * N] * silu(acc[:, j * N : (j + 1) * N].astype(BF).astype(F32))
        square = square + jnp.sum(g * g, axis=1, keepdims=True)
        gated.append(g)
    scale = lax.rsqrt(square / ZC + 1e-05)
    for j in range(XT):
        normed[:, j * N : (j + 1) * N] = (gated[j] * scale * gain_ref[0:1, j * N : (j + 1) * N]).astype(BF)

    ring_o.shared(0)

    @pl.loop(1, half - 1)
    def _(k):
        ring_o.shared(k)

    def hand(src, dst, along, place, send_sem, recv_sem):
        there = (y_at * side + place, s) if along == 0 else (place * side + x_at, s)
        return pltpu.make_async_remote_copy(
            src_ref=src, dst_ref=dst, send_sem=send_sem, recv_sem=recv_sem,
            device_id=there, device_id_type=MESH,
        )

    at = (x_at, y_at)

    def term(yo, xo, q):
        w = jnp.concatenate([buf_o[q, 0], buf_o[q, 1]], axis=1)
        value = jnp.dot(normed[...], w, preferred_element_type=F32).astype(BF)
        for h, (to, index) in enumerate(((xo, yo), (yo, xo))):
            part = value[h * HALF : (h + 1) * HALF]
            t_out[h, to, index] = part

            @pl.when(to != at[h])
            def _():
                hand(
                    t_out.at[h, to, index], r_in.at[h, at[h], index], h, to,
                    rs_send.at[h], rs_recv.at[h],
                ).start()

            @pl.when(to == at[h])
            def _():
                r_in[h, to, index] = part

    def terms(of_last_steps):
        @pl.loop(0, n_dp)
        def _(i):
            yo, xo = lax.rem(y_at + 1 + i // side, side), lax.rem(x_at + 1 + i, side)
            q = lax.rem(z - (yo * side + xo) + 2 * chips, chips)
            late = (q >= half - 1) & (q <= half + 1)

            @pl.when(late if of_last_steps else ~late)
            def _():
                term(yo, xo, q)

    terms(False)
    ring_o.step(half)
    ring_o.shared(half - 1)
    ring_o.shared(half)
    terms(True)

    few = pl.ds(0, side - 1)
    for h in range(2):
        first_stage = hand(t_out.at[h, few], r_in.at[h, few], h, at[h], rs_send.at[h], rs_recv.at[h])
        first_stage.wait_recv()
        for j in range(1, side + 1):
            to = lax.rem(at[1 - h] + j, side)
            partial = jnp.zeros((HALF, 2 * N), F32)
            for e in range(side):
                partial = partial + r_in[h, e, to].astype(F32)
            p_out[h, to] = partial.astype(BF)
            if j < side:
                hand(
                    p_out.at[h, to], p_in.at[h, at[1 - h]], 1 - h, to, rs_send.at[2 + h], rs_recv.at[2 + h]
                ).start()
            else:
                p_in[h, to] = partial.astype(BF)
    for h in range(2):
        second_stage = hand(
            p_out.at[h, few], p_in.at[h, few], h, at[h], rs_send.at[2 + h], rs_recv.at[2 + h]
        )
        second_stage.wait_recv()
        total = jnp.zeros((HALF, 2 * N), F32)
        for e in range(side):
            total = total + p_in[h, e].astype(F32)
        out_ref[h * HALF : (h + 1) * HALF] = total.astype(BF)
        second_stage.wait_send()
        hand(t_out.at[h, few], r_in.at[h, few], h, at[h], rs_send.at[h], rs_recv.at[h]).wait_send()
    halo.wait_send()
    swap1.wait_send()
    swap2.wait_send()
    gather_fades.drain()
    gather_states.drain()
    return_states.drain()
    ring_a.drain()
    ring_z.drain()
    ring_o.drain()


def per_device(
    tokens, w_in, conv_weight, conv_bias, dt_bias, decay_rate, skip_gain, norm_gain, w_out
):
    chips, n_dp = lax.axis_size("seq") // 2, lax.axis_size("dp")
    tile_rows = 2 * N // chips
    side = math.isqrt(n_dp)
    dma = pltpu.SemaphoreType.DMA
    vmem = pl.BlockSpec(memory_space=pltpu.VMEM)
    return pl.pallas_call(
        functools.partial(mixer_kernel, chips, n_dp),
        out_shape=jax.ShapeDtypeStruct((BLOCK, 2 * N), BF),
        in_specs=[pl.BlockSpec(memory_space=pl.ANY), vmem] + [pl.BlockSpec(memory_space=pl.ANY)] * 7,
        out_specs=vmem,
        scratch_shapes=[
            pltpu.VMEM((KCONV, XG), F32),
            pltpu.VMEM((1, XG), F32),
            pltpu.VMEM((1, HG), F32),
            pltpu.VMEM((1, HG), F32),
            pltpu.VMEM((1, HG), F32),
            pltpu.VMEM((1, ZC), F32),
            pltpu.VMEM(tokens.shape, BF),
            pltpu.VMEM((chips, 2, AROWS, N), BF),
            pltpu.VMEM((chips, 2, ZC, N), BF),
            pltpu.VMEM((chips, 2, ZC, N), BF),
            pltpu.VMEM((BLOCK, ZC + XG), F32),
            pltpu.VMEM((BLOCK, 16), F32),
            pltpu.VMEM((HALO + BLOCK, XG), F32),
            pltpu.VMEM((N + 16, 2 * N), BF),
            pltpu.VMEM((N + 16, 2 * N), BF),
            pltpu.VMEM((chips, tile_rows, N), BF),
            pltpu.VMEM((chips, tile_rows, N), BF),
            pltpu.VMEM((chips, 1, N), F32),
            pltpu.VMEM((chips, 1, N), F32),
            pltpu.VMEM((N, 2 * N), F32),
            pltpu.VMEM((1, 2 * N), F32),
            pltpu.VMEM((BLOCK, N), BF),
            pltpu.VMEM((BLOCK, HG), F32),
            pltpu.VMEM((BLOCK, ZC), F32),
            pltpu.VMEM((chips, tile_rows, N), BF),
            pltpu.VMEM((chips, tile_rows, N), BF),
            pltpu.VMEM((N, 2 * N), BF),
            pltpu.VMEM((2, N, 2 * N), BF),
            pltpu.VMEM((BLOCK, ZC), BF),
            pltpu.VMEM((2, side, side, HALF, 2 * N), BF),
            pltpu.VMEM((2, side, side, HALF, 2 * N), BF),
            pltpu.VMEM((2, side, HALF, 2 * N), BF),
            pltpu.VMEM((2, side, HALF, 2 * N), BF),
            dma((8,)), dma, dma, dma, dma, dma, dma,
            dma, dma, dma, dma, dma, dma, dma((4,)), dma((4,)),
            *ring_sems(chips, A_PARTS),
            *ring_sems(chips, W_PARTS),
            *ring_sems(chips, W_PARTS),
        ],
        compiler_params=pltpu.CompilerParams(
            collective_id=0, has_side_effects=True, vmem_limit_bytes=VMEM_LIMIT
        ),
    )(
        tokens, w_in.T, conv_weight, conv_bias, dt_bias[None], decay_rate[None], skip_gain[None],
        norm_gain[None], w_out,
    )


def solution(mesh):
    placed = (
        P("seq", None),
        P("seq", "dp"),
        P(None, "dp"),
        P("dp"),
        P("dp"),
        P("dp"),
        P("dp"),
        P("dp"),
        P("dp", "seq"),
    )
    return jax.shard_map(
        per_device, mesh=mesh, in_specs=placed, out_specs=P("seq", "dp"), check_vma=False
    )
```
